512 devices in a mesh: grp: 2 (over core), seq: 64 (over y, x, z_lo), tp: 4 (over z_hi).
Axes of the slice: x: 4, y: 4, z: 16 (z_hi: 4, z_lo: 4; z = z_hi * 4 + z_lo), core: 2. Of those that a mesh axis runs over, the one named last changes fastest.
Arguments:
- prompt_queries: bfloat16 [2, 8192, 4096], P('grp', 'seq', 'tp'), may hold values from -6 to 6
- prompt_keys: bfloat16 [2, 8192, 512], P('grp', 'seq', 'tp'), may hold values from -6 to 6
- prefill_value_rows: bfloat16 [2, 8192, 512], P('grp', 'seq', 'tp'), may hold values from -6 to 6
- step_queries: bfloat16 [2, 2, 64, 4096], P('grp', None, None, 'tp'), may hold values from -6 to 6
- step_keys: bfloat16 [2, 2, 64, 512], P('grp', None, None, 'tp'), may hold values from -6 to 6
- decode_step_values: bfloat16 [2, 2, 64, 512], P('grp', None, None, 'tp'), may hold values from -6 to 6
- context_lengths: int32 [2, 64], P('grp'), may hold values from 1 to 8192, as said below
- span_order: int32 [2, 128], replicated, may hold values from 0 to 127, each once within a row
- page_owner: int32 [2, 4096, 1], replicated, may hold values from 0 to 63; in each aligned block of 64 rows (0 to 63, 64 to 127, ..., all dimensions but the last counted through in order) at most 2 rows name the same one
Outputs:
- prompt_attended: bfloat16 [2, 8192, 4096], P('grp', 'seq', 'tp')
- step_attended: bfloat16 [2, 2, 64, 4096], P('grp', None, 'seq', 'tp')
The draws below stay inside these ranges and needn't reach their ends.
Inputs may be any that keep to these rules, and one draw needn't show every extreme that they name: `context_lengths`: each pool has a row that reads all 8192 entries. `span_order`: each row is a permutation of 0 to 127. `page_owner`: within the 64 pages of one device (aligned blocks of pages), no owner is named by more than 2 pages, a bound that some block reaches.
All inputs are finite; a program needn't handle non-finite values.
Results may differ from the reference program's by a relative error of at most 0.009.
Values may be sent and summed in bfloat16 or wider, within the bound.
No kernel may reach another device: no remote copies, remote signals or barrier semaphores. Data moves between devices by JAX's collectives and lax.ppermute only.
A program may use at most 192 MiB of HBM per device.

```python
import math
import jax
import jax.numpy as jnp
import numpy as np
from jax import lax

QUERY_HEADS = 32
KEY_VALUE_HEADS = 4
HEAD_SIZE = 128
DEVICE_TOKENS = 128
POOL_ROWS = 64
DECODE_STEPS = 2
PAGE_TOKENS = 2
REQUEST_TOKENS = 8192
NBLOCKS = 128
PAGES_DEV = 64
REQUEST_PAGES = 4096
CAP = 2
N_SEQ = 64


def draw_prompt_keys(key, part):
    own_key = jax.random.fold_in(key, 11)
    count_of_rows = 2 * REQUEST_TOKENS
    width_of_row = KEY_VALUE_HEADS * HEAD_SIZE
    drawn = jnp.clip(jax.random.normal(own_key, (count_of_rows, width_of_row)), -6.0, 6.0)
    return drawn.reshape(2, REQUEST_TOKENS, width_of_row).astype(jnp.bfloat16)


def draw_prompt_queries(key, part):
    own_key = jax.random.fold_in(key, 13)
    count_of_rows = 2 * REQUEST_TOKENS
    width_of_row = QUERY_HEADS * HEAD_SIZE
    drawn = jnp.clip(jax.random.normal(own_key, (count_of_rows, width_of_row)), -6.0, 6.0)
    return drawn.reshape(2, REQUEST_TOKENS, width_of_row).astype(jnp.bfloat16)


def draw_step_keys(key, part):
    own_key = jax.random.fold_in(key, 17)
    width_of_row = KEY_VALUE_HEADS * HEAD_SIZE
    drawn = jnp.clip(jax.random.normal(own_key, (2, DECODE_STEPS, POOL_ROWS, width_of_row)), -6.0, 6.0)
    return drawn.astype(jnp.bfloat16)


def draw_step_queries(key, part):
    own_key = jax.random.fold_in(key, 19)
    width_of_row = QUERY_HEADS * HEAD_SIZE
    drawn = jnp.clip(jax.random.normal(own_key, (2, DECODE_STEPS, POOL_ROWS, width_of_row)), -6.0, 6.0)
    return drawn.astype(jnp.bfloat16)


def draw_context_lengths(key, part):
    own_key = jax.random.fold_in(key, 31)
    length_key, longest_key = jax.random.split(own_key)
    drawn = jax.random.randint(length_key, (2, POOL_ROWS), 1, REQUEST_TOKENS + 1)
    longest = jax.random.randint(longest_key, (2, 1), 0, POOL_ROWS)
    return jnp.where(jnp.arange(POOL_ROWS)[None, :] == longest, REQUEST_TOKENS, drawn).astype(jnp.int32)


def shard_levels(rng, dims, cuts, smallest, high):
    def one(position, parts):
        draws = jax.random.uniform(jax.random.fold_in(jax.random.fold_in(rng, 6), position), (parts,), jnp.float32, smallest / len(cuts), high / len(cuts))
        return jnp.repeat(jnp.exp(draws), dims[position] // parts).reshape((-1,) + (1,) * (len(dims) - position - 1))

    loudness = one(*cuts[0])
    for cut in cuts[1:]:
        loudness = loudness * one(*cut)
    return loudness


def routed_block(stream_key, own, number, rows, count, top, limit, slope):
    ranking = jax.random.permutation(stream_key, count)
    heavy_load, usual = shares(count, rows * top, limit, slope, True), shares(count, rows * top, limit, slope, False)
    places = jnp.arange(count)

    def named(sizes, turn):
        used = int((sizes > 0).sum())
        fixed = max(1, used // 4)
        shifted = fixed + (places - fixed + turn * (used - fixed)) % max(1, count - fixed)
        return jnp.zeros((count,), jnp.int32).at[ranking[jnp.where(places < fixed, places, shifted)]].set(jnp.asarray(sizes, jnp.int32))

    sizes = jnp.where(number % 4 == 0, named(heavy_load, number // 4), named(usual, number - number // 4 - 1))
    mixed = jax.random.permutation(jax.random.fold_in(own, 3), count)
    donor, receiver = mixed[0:count // 2 * 2:2], mixed[1:count // 2 * 2:2]
    margin = jnp.minimum(sizes[donor] - 1, limit - sizes[receiver]) // 2
    margin = jnp.where((donor == ranking[0]) | (receiver == ranking[0]) | (sizes[receiver] == 0), 0, jnp.maximum(margin, 0))
    shifted = jax.random.randint(jax.random.fold_in(own, 4), (count // 2,), 0, 1 << 20) % (margin + 1)
    sizes = sizes.at[donor].add(-shifted).at[receiver].add(shifted)
    items = jnp.searchsorted(jnp.cumsum(sizes), jnp.arange(rows * top), side="right").astype(jnp.int32)
    table = items.reshape(top, rows).T
    table = table[jax.random.permutation(jax.random.fold_in(own, 1), rows)]
    turn = jax.random.randint(jax.random.fold_in(own, 2), (rows, 1), 0, top)
    return jnp.take_along_axis(table, (jnp.arange(top)[None, :] + turn) % top, axis=1)


def shares(number_of, total, most, lean, full):
    loads = [(1 << 20) // math.isqrt(rank ** lean) + 1 for rank in range(1, number_of + 1)]
    largest = most if full else min(most, max(-(-total // number_of), total * loads[0] // sum(loads)))
    least = 1 if total - largest >= number_of - 1 else 0
    given, rest = [largest] + [least] * (number_of - 1), total - largest - least * (number_of - 1)
    while rest > 0:
        free = [i for i in range(1, number_of) if given[i] < largest] or [i for i in range(1, number_of) if given[i] < most]
        mass, left = sum([loads[i] for i in free]), rest
        for i in free:
            addition = min(most - given[i], max(1, left * loads[i] // mass), rest)
            given[i] = given[i] + addition
            rest = rest - addition
    return np.array(given)


def centred(rng, extent, spread, reach, cuts=(), held_as=jnp.bfloat16):
    result = spread * jax.random.normal(rng, extent, jnp.float32)
    if cuts:
        result = result * shard_levels(rng, extent, cuts, -0.22, 0.18)
    return jnp.clip(result, -reach, reach).astype(held_as)


def setup_inputs(seed: int = 0) -> dict:
    arg_keys = jax.random.split(jax.random.key(seed), 10)
    prompt_queries = draw_prompt_queries(jax.random.fold_in(arg_keys[9], 71), 0)
    prompt_keys = draw_prompt_keys(jax.random.fold_in(arg_keys[9], 71), 0)
    prefill_value_rows = centred(arg_keys[2], (2, REQUEST_TOKENS, KEY_VALUE_HEADS * HEAD_SIZE), 1.0, 6.0, ((0, 2), (1, 64), (2, 4)))
    step_queries = draw_step_queries(jax.random.fold_in(arg_keys[9], 71), 0)
    step_keys = draw_step_keys(jax.random.fold_in(arg_keys[9], 71), 0)
    decode_step_values = centred(arg_keys[5], (2, DECODE_STEPS, POOL_ROWS, KEY_VALUE_HEADS * HEAD_SIZE), 1.0, 6.0, ((0, 2), (3, 4)))
    context_lengths = draw_context_lengths(jax.random.fold_in(arg_keys[9], 71), 0)
    span_order = jax.vmap(lambda own: jax.random.permutation(own, NBLOCKS))(jax.random.split(arg_keys[7], 2)).reshape((2, NBLOCKS)).astype(jnp.int32)
    page_owner_keys = jax.random.split(jax.random.fold_in(arg_keys[8], 1), 2 * REQUEST_PAGES // PAGES_DEV)
    page_owner_turns = jax.random.permutation(jax.random.fold_in(arg_keys[8], 3), 2 * REQUEST_PAGES // PAGES_DEV)
    page_owner = jax.vmap(lambda own, number: routed_block(jax.random.fold_in(arg_keys[8], 2), own, number, PAGES_DEV, N_SEQ, 1, CAP, 2))(page_owner_keys, page_owner_turns).reshape((2, REQUEST_PAGES, 1))
    return dict(prompt_queries=prompt_queries, prompt_keys=prompt_keys, prefill_value_rows=prefill_value_rows, step_queries=step_queries, step_keys=step_keys, decode_step_values=decode_step_values, context_lengths=context_lengths, span_order=span_order, page_owner=page_owner)


NEG_FILL = -1.0e30


def storage_positions(order_row, half_rows):
    offsets = jnp.arange(half_rows, dtype=jnp.int32)
    return (order_row[:, None].astype(jnp.int32) * half_rows + offsets[None, :]).reshape(-1)


def masked_softmax(scores, allowed, product):
    scores = jnp.where(allowed, scores, NEG_FILL)
    maximum = jnp.max(scores, axis=-1, keepdims=True)
    weights = jnp.where(allowed, jnp.exp(scores - maximum), 0.0)
    totals = jnp.sum(weights, axis=-1, keepdims=True)
    rounded = lax.optimization_barrier(weights.astype(jnp.bfloat16)).astype(jnp.float32)
    return product(rounded) / totals


def prefill_pool(query_tile, key_tile, value_tile, order_row):
    positions = storage_positions(order_row, DEVICE_TOKENS // 2)
    query_group_width = QUERY_HEADS // KEY_VALUE_HEADS
    key_tensor_three = key_tile.reshape(REQUEST_TOKENS, KEY_VALUE_HEADS, HEAD_SIZE).astype(jnp.float32)
    value_tensor_three = value_tile.reshape(REQUEST_TOKENS, KEY_VALUE_HEADS, HEAD_SIZE).astype(jnp.float32)
    query_tensor_five = query_tile.reshape(N_SEQ, DEVICE_TOKENS, KEY_VALUE_HEADS, query_group_width, HEAD_SIZE)
    query_pos = positions.reshape(N_SEQ, DEVICE_TOKENS)

    def one_block(block_args):
        block_rows, block_pos = block_args
        scores = jnp.einsum("tgjd,ngd->gjtn", block_rows.astype(jnp.float32), key_tensor_three) * (HEAD_SIZE ** -0.5)
        allowed = positions[None, None, None, :] <= block_pos[None, None, :, None]
        allowed = jnp.broadcast_to(allowed, scores.shape)
        attended = masked_softmax(scores, allowed, lambda rounded: jnp.einsum("gjtn,ngd->gjtd", rounded, value_tensor_three))
        return attended.transpose(2, 0, 1, 3).reshape(DEVICE_TOKENS, QUERY_HEADS * HEAD_SIZE)

    output_rows = lax.map(one_block, (query_tensor_five, query_pos))
    return output_rows.reshape(REQUEST_TOKENS, QUERY_HEADS * HEAD_SIZE).astype(jnp.bfloat16)


def decode_pool(fresh_queries, fresh_keys, fresh_values, lengths, key_tile, value_tile, owner_row):
    query_group_width = QUERY_HEADS // KEY_VALUE_HEADS
    page_sequence = jnp.argsort(owner_row, stable=True)
    cached_key_rows = key_tile.reshape(REQUEST_PAGES, PAGE_TOKENS, KEY_VALUE_HEADS * HEAD_SIZE)[page_sequence].reshape(REQUEST_TOKENS, KEY_VALUE_HEADS, HEAD_SIZE).astype(jnp.float32)
    cached_value_rows = value_tile.reshape(REQUEST_PAGES, PAGE_TOKENS, KEY_VALUE_HEADS * HEAD_SIZE)[page_sequence].reshape(REQUEST_TOKENS, KEY_VALUE_HEADS, HEAD_SIZE).astype(jnp.float32)
    query_tensor_five = fresh_queries.reshape(DECODE_STEPS, POOL_ROWS, KEY_VALUE_HEADS, query_group_width, HEAD_SIZE).astype(jnp.float32)
    key_tensor_four = fresh_keys.reshape(DECODE_STEPS, POOL_ROWS, KEY_VALUE_HEADS, HEAD_SIZE).astype(jnp.float32)
    value_tensor_four = fresh_values.reshape(DECODE_STEPS, POOL_ROWS, KEY_VALUE_HEADS, HEAD_SIZE).astype(jnp.float32)
    scale = HEAD_SIZE ** -0.5
    cache_scores = jnp.einsum("sbgjd,ngd->sbgjn", query_tensor_five, cached_key_rows) * scale
    own_scores = jnp.einsum("sbgjd,ubgd->sbgju", query_tensor_five, key_tensor_four) * scale
    entry_index = jnp.arange(REQUEST_TOKENS, dtype=jnp.int32)
    cache_ok = entry_index[None, None, None, None, :] < lengths.astype(jnp.int32)[None, :, None, None, None]
    cache_ok = jnp.broadcast_to(cache_ok, cache_scores.shape)
    step_range = jnp.arange(DECODE_STEPS, dtype=jnp.int32)
    own_ok = (step_range[None, :] <= step_range[:, None])[:, None, None, None, :]
    own_ok = jnp.broadcast_to(own_ok, own_scores.shape)
    scores = jnp.concatenate([cache_scores, own_scores], axis=-1)
    allowed = jnp.concatenate([cache_ok, own_ok], axis=-1)

    def product(rounded):
        cache_part = jnp.einsum("sbgjn,ngd->sbgjd", rounded[..., :REQUEST_TOKENS], cached_value_rows)
        own_part = jnp.einsum("sbgju,ubgd->sbgjd", rounded[..., REQUEST_TOKENS:], value_tensor_four)
        return cache_part + own_part

    attended = masked_softmax(scores, allowed, product)
    return attended.reshape(DECODE_STEPS, POOL_ROWS, QUERY_HEADS * HEAD_SIZE).astype(jnp.bfloat16)


def reference(prompt_queries, prompt_keys, prefill_value_rows, step_queries, step_keys, decode_step_values, context_lengths, span_order, page_owner):
    prompt_attended = jnp.stack([prefill_pool(prompt_queries[pool_index], prompt_keys[pool_index], prefill_value_rows[pool_index], span_order[pool_index]) for pool_index in range(2)])
    step_attended = jnp.stack([decode_pool(step_queries[pool_index], step_keys[pool_index], decode_step_values[pool_index], context_lengths[pool_index], prompt_keys[1 - pool_index], prefill_value_rows[1 - pool_index], page_owner[1 - pool_index, :, 0]) for pool_index in range(2)])
    return prompt_attended, step_attended
```

```python
import functools
import math

import jax
import jax.numpy as jnp
from jax import lax
from jax.experimental import pallas as pl
from jax.experimental.pallas import tpu as pltpu
from jax.sharding import Mesh, PartitionSpec as P

HEAD = 128
HALF = 64
GROUP = 8
SIDE = 4
PROMPT_ROWS = 2 * GROUP * HALF
DECODE_ROWS = 16
ROWS = PROMPT_ROWS + DECODE_ROWS
ROW_TILE = 208
NEG = -1e30
SCALE2 = math.log2(math.e) / math.sqrt(HEAD)
VMEM_BYTES = 40 * 1024 * 1024

VMEM = pl.BlockSpec(memory_space=pltpu.VMEM)
SMEM = pl.BlockSpec(memory_space=pltpu.SMEM)
NT = (((1,), (1,)), ((), ()))


def params():
    return pltpu.CompilerParams(vmem_limit_bytes=VMEM_BYTES)


def cost(keys):
    return pl.CostEstimate(
        flops=4 * ROWS * keys * 256,
        bytes_accessed=keys * 512 + ROWS * 4096,
        transcendentals=ROWS * keys,
    )


def seq_position():
    return lax.axis_index("y"), lax.axis_index("x"), lax.axis_index("z")


def pack_kernel(queries, keys, values, lengths, message, rows):
    y, x, z = seq_position()
    mine = (y * SIDE + x) * SIDE + z
    rows[...] = jnp.zeros_like(rows)
    for step in range(2):
        block = queries[0, step].astype(jnp.float32)
        here = lax.broadcasted_iota(jnp.int32, block.shape, 0) == mine
        line = jnp.sum(jnp.where(here, block, 0.0), axis=0, keepdims=True)
        for head in range(GROUP):
            rows[step * GROUP + head : step * GROUP + head + 1, :] = line[
                :, head * HEAD : (head + 1) * HEAD
            ]
        for source, first in ((keys, 16), (values, 32)):
            block = source[0, step].astype(jnp.float32)
            here = lax.broadcasted_iota(jnp.int32, block.shape, 0) == mine
            rows[first + step : first + step + 1, :] = jnp.sum(
                jnp.where(here, block, 0.0), axis=0, keepdims=True
            )
    length = lengths[0, mine]
    lane = lax.broadcasted_iota(jnp.int32, (1, HEAD), 1)
    digits = jnp.where(lane == 0, length >> 7, jnp.where(lane == 1, length & 127, 0))
    rows[47:48, :] = digits.astype(jnp.float32)
    message[...] = rows[...].astype(jnp.bfloat16)


def init_kernel(queries, own_kv, message, owners, q_aug, top, acc, entry_bias):
    lane = lax.broadcasted_iota(jnp.int32, (HALF, HEAD), 1)
    for block in range(2):
        tag = jnp.where(lane == 64 + block, 1.0, 0.0).astype(jnp.bfloat16)
        for head in range(GROUP):
            at = (block * GROUP + head) * HALF
            q_aug[at : at + HALF, 0:HEAD] = queries[
                0, block * HALF : (block + 1) * HALF, head * HEAD : (head + 1) * HEAD
            ]
            q_aug[at : at + HALF, HEAD : 2 * HEAD] = tag
    lane16 = lax.broadcasted_iota(jnp.int32, (DECODE_ROWS, HEAD), 1)
    q_aug[PROMPT_ROWS:ROWS, 0:HEAD] = message[0:16, :]
    q_aug[PROMPT_ROWS:ROWS, HEAD : 2 * HEAD] = jnp.where(lane16 < 64, 1.0, 0.0).astype(jnp.bfloat16)

    def begin(first, count, key_rows, value_rows, allowed):
        scores = lax.dot_general(
            q_aug[first : first + count, 0:HEAD], key_rows, NT, preferred_element_type=jnp.float32
        )
        scores = jnp.where(allowed, scores, NEG)
        best = jnp.max(scores, axis=1, keepdims=True)
        weights = jnp.where(allowed, jnp.exp2((scores - best) * SCALE2), 0.0)
        total = jnp.sum(weights, axis=1, keepdims=True)
        top[first : first + count, :] = jnp.broadcast_to(best, (count, HEAD))
        acc[first : first + count, 0:HEAD] = jnp.dot(
            weights.astype(jnp.bfloat16), value_rows, preferred_element_type=jnp.float32
        )
        acc[first : first + count, HEAD : 2 * HEAD] = jnp.broadcast_to(total, (count, HEAD))

    span = GROUP * HALF
    token = lax.broadcasted_iota(jnp.int32, (span, HALF), 0) & (HALF - 1)
    column = lax.broadcasted_iota(jnp.int32, (span, HALF), 1)
    for block in range(2):
        begin(
            block * span, span, own_kv[block, :, 0:HEAD], own_kv[block, :, HEAD : 2 * HEAD], column <= token
        )
    step = lax.broadcasted_iota(jnp.int32, (16, 16), 0) >> 3
    begin(
        PROMPT_ROWS,
        DECODE_ROWS,
        message[16:32, :],
        message[32:48, :],
        lax.broadcasted_iota(jnp.int32, (16, 16), 1) <= step,
    )

    digits = message[32:48, :].astype(jnp.float32)
    last = lax.broadcasted_iota(jnp.int32, (16, HEAD), 0) == 15
    digit_worth = jnp.where(lane16 == 0, 128.0, jnp.where(lane16 == 1, 1.0, 0.0))
    length = jnp.sum(jnp.where(last, digits * digit_worth, 0.0), axis=(0, 1), keepdims=True)
    length = length.astype(jnp.int32)
    page = lax.broadcasted_iota(jnp.int32, (64, 64), 0) * 64 + lax.broadcasted_iota(
        jnp.int32, (64, 64), 1
    )
    rank_key = owners[...] * 4096 + page
    wanted = [((length + 1) >> 1).astype(jnp.float32), (length >> 1).astype(jnp.float32)]
    bound = [jnp.zeros((1, 1), jnp.int32), jnp.zeros((1, 1), jnp.int32)]
    for bit in range(18, -1, -1):
        for odd in range(2):
            trial = bound[odd] + (1 << bit)
            below = jnp.sum(jnp.where(rank_key < trial, 1.0, 0.0), axis=(0, 1), keepdims=True)
            bound[odd] = jnp.where(below <= wanted[odd], trial, bound[odd])
    token = lax.broadcasted_iota(jnp.int32, (2 * HALF, 64), 0)
    of_page = lax.broadcasted_iota(jnp.int32, (2 * HALF, 64), 1)
    allowed = jnp.zeros((2 * HALF, 64), jnp.float32)
    for odd in range(2):
        spread = jnp.where(token == 2 * of_page + odd, 1.0, 0.0).astype(jnp.bfloat16)
        read = jnp.where(rank_key < bound[odd], 1.0, 0.0).astype(jnp.bfloat16)
        allowed += lax.dot_general(spread, read, NT, preferred_element_type=jnp.float32)
    bias = (1.0 - allowed) * NEG
    entry_bias[...] = jnp.concatenate([bias, jnp.zeros_like(bias)], axis=1)


def chunk_kernel(layout, final, key_tile, *refs):
    order, entry_bias, q_aug, top_in, acc_in = refs[:5]
    pieces = refs[5 : 5 + len(layout)]
    outs = refs[5 + len(layout) :]
    if final:
        prompt_out, decode_out, top, acc, k_aug, v_aug = outs
    else:
        top, acc, k_aug, v_aug = outs
    y, x, z = seq_position()
    pool = lax.axis_index("grp")
    mine = (y * SIDE + x) * SIDE + z
    limits = (order[pool, 2 * mine], order[pool, 2 * mine + 1])
    lane = lax.broadcasted_iota(jnp.int32, (HALF, HEAD), 1)
    ones = jnp.ones((HALF, HEAD), jnp.bfloat16)
    slot = 0
    for piece, blocks in zip(pieces, layout):
        for index, source, half in blocks(y, x, z):
            at = order[pool, 2 * source + half]
            bias = [jnp.where(at < limit, 0.0, NEG) for limit in limits]
            masks = jnp.where(
                lane == source,
                entry_bias[half * HALF : (half + 1) * HALF, :],
                jnp.where(lane == 64, bias[0], jnp.where(lane == 65, bias[1], 0.0)),
            )
            rows = slice(slot * HALF, (slot + 1) * HALF)
            k_aug[rows, 0:HEAD] = piece[index][:, 0:HEAD]
            k_aug[rows, HEAD : 2 * HEAD] = masks.astype(jnp.bfloat16)
            v_aug[rows, 0:HEAD] = piece[index][:, HEAD : 2 * HEAD]
            v_aug[rows, HEAD : 2 * HEAD] = ones
            slot += 1
    top[...] = top_in[...]
    acc[...] = acc_in[...]

    def step(tile, carry):
        keys = pl.ds(pl.multiple_of(tile * key_tile, key_tile), key_tile)
        for first in range(0, ROWS, ROW_TILE):
            rows = slice(first, first + ROW_TILE)
            scores = lax.dot_general(
                q_aug[rows, :], k_aug[keys, :], NT, preferred_element_type=jnp.float32
            )
            old = top[rows, :]
            best = jnp.maximum(old, jnp.max(scores, axis=1, keepdims=True))
            shrink = jnp.exp2((old - best) * SCALE2)
            weights = jnp.exp2((scores - best[:, 0:1]) * SCALE2).astype(jnp.bfloat16)
            product = jnp.dot(weights, v_aug[keys, :], preferred_element_type=jnp.float32)
            top[rows, :] = best
            acc[rows, 0:HEAD] = acc[rows, 0:HEAD] * shrink + product[:, 0:HEAD]
            acc[rows, HEAD : 2 * HEAD] = acc[rows, HEAD : 2 * HEAD] * shrink + product[:, HEAD : 2 * HEAD]
        return carry

    lax.fori_loop(0, slot * HALF // key_tile, step, 0)
    if final:
        for block in range(2):
            for head in range(GROUP):
                at = (block * GROUP + head) * HALF
                prompt_out[0, block * HALF : (block + 1) * HALF, head * HEAD : (head + 1) * HEAD] = (
                    acc[at : at + HALF, 0:HEAD] / acc[at : at + HALF, HEAD : 2 * HEAD]
                ).astype(jnp.bfloat16)
        decode_out[...] = (
            acc[PROMPT_ROWS:ROWS, 0:HEAD] / acc[PROMPT_ROWS:ROWS, HEAD : 2 * HEAD]
        ).astype(jnp.bfloat16)


def device_of(y, x, z):
    return (y * SIDE + x) * SIDE + z


def back(at, by):
    return (at + SIDE - by) & (SIDE - 1)


def run_chunk(layout, pieces, order, entry_bias, q_aug, state, final=False, key_tile=512):
    blocks = sum(len(make(0, 0, 0)) for make in layout)
    keys = blocks * HALF
    state_shapes = [
        jax.ShapeDtypeStruct((ROWS, HEAD), jnp.float32),
        jax.ShapeDtypeStruct((ROWS, 2 * HEAD), jnp.float32),
    ]
    scratch = [
        pltpu.VMEM((keys, 2 * HEAD), jnp.bfloat16),
        pltpu.VMEM((keys, 2 * HEAD), jnp.bfloat16),
    ]
    if final:
        out_shape = [
            jax.ShapeDtypeStruct((1, 2 * HALF, GROUP * HEAD), jnp.bfloat16),
            jax.ShapeDtypeStruct((DECODE_ROWS, HEAD), jnp.bfloat16),
        ]
        scratch = [
            pltpu.VMEM((ROWS, HEAD), jnp.float32),
            pltpu.VMEM((ROWS, 2 * HEAD), jnp.float32),
        ] + scratch
    else:
        out_shape = state_shapes
    return pl.pallas_call(
        functools.partial(chunk_kernel, layout, final, key_tile),
        out_shape=out_shape,
        in_specs=[SMEM] + [VMEM] * (4 + len(pieces)),
        out_specs=[VMEM] * len(out_shape),
        scratch_shapes=scratch,
        compiler_params=params(),
        cost_estimate=cost(keys),
    )(order, entry_bias, q_aug, *state, *pieces)


def rotate(block, axis, by):
    return lax.ppermute(block, axis, [(i, (i + by) % SIDE) for i in range(SIDE)])


def gather_all(block, axis):
    copies = jnp.broadcast_to(block[None], (SIDE,) + block.shape)
    return lax.all_to_all(copies, axis, split_axis=0, concat_axis=0, tiled=True)


def per_device(
    prompt_queries,
    prompt_keys,
    prefill_value_rows,
    step_queries,
    step_keys,
    decode_step_values,
    context_lengths,
    span_order,
    page_owner,
):
    kv = jnp.concatenate([prompt_keys[0], prefill_value_rows[0]], axis=1)
    kv = kv.reshape(2, HALF, 2 * HEAD)
    z_parts = [kv] + [rotate(kv, "z", by) for by in (1, 2, 3)]
    message = pl.pallas_call(
        pack_kernel,
        out_shape=jax.ShapeDtypeStruct((48, HEAD), jnp.bfloat16),
        in_specs=[VMEM, VMEM, VMEM, SMEM],
        out_specs=VMEM,
        scratch_shapes=[pltpu.VMEM((48, HEAD), jnp.float32)],
        compiler_params=params(),
    )(step_queries, step_keys, decode_step_values, context_lengths)
    message = lax.ppermute(message, "grp", [(0, 1), (1, 0)])
    pool = lax.axis_index("grp")
    owners = lax.dynamic_index_in_dim(page_owner, pool, 0, keepdims=False).reshape(64, 64)

    z_first = jnp.stack([part[0] for part in z_parts])
    z_second = jnp.stack([part[1] for part in z_parts])

    first_x = gather_all(z_first, "x")
    second_y = [z_second] + [rotate(z_second, "y", by) for by in (1, 2, 3)]
    low = jnp.stack([second_y[0], second_y[1]])
    high = jnp.stack([second_y[2], second_y[3]])

    first_y = gather_all(first_x, "y")
    low_left = rotate(low, "x", 1)
    high_right = rotate(high, "x", 3)
    high_left = rotate(high, "x", 1)
    low_right = rotate(low, "x", 3)
    low_far = rotate(low_left, "x", 1)
    high_far = rotate(high_right, "x", 3)

    q_aug, top, acc, entry_bias = pl.pallas_call(
        init_kernel,
        out_shape=[
            jax.ShapeDtypeStruct((ROWS, 2 * HEAD), jnp.bfloat16),
            jax.ShapeDtypeStruct((ROWS, HEAD), jnp.float32),
            jax.ShapeDtypeStruct((ROWS, 2 * HEAD), jnp.float32),
            jax.ShapeDtypeStruct((2 * HALF, HEAD), jnp.float32),
        ],
        in_specs=[VMEM] * 4,
        out_specs=[VMEM] * 4,
        compiler_params=params(),
        cost_estimate=cost(512),
    )(prompt_queries, kv, message, owners)

    def first_blocks(shifts):
        def make(y, x, z):
            return [
                ((back(y, by), at_x, by_z), device_of(back(y, by), at_x, back(z, by_z)), 0)
                for by in shifts
                for at_x in range(SIDE)
                for by_z in range(SIDE)
            ]

        return make

    def first_plane(y, x, z):
        return [
            ((at_x, by_z), device_of(y, at_x, back(z, by_z)), 0)
            for at_x in range(SIDE)
            for by_z in range(SIDE)
        ]

    def second_blocks(by_x, shifts):
        def make(y, x, z):
            return [
                ((place, by_z), device_of(back(y, by_y), back(x, by_x), back(z, by_z)), 1)
                for place, by_y in enumerate(shifts)
                for by_z in range(SIDE)
            ]

        return make

    low_at, high_at = (0, 1), (2, 3)
    fixed = (span_order, entry_bias, q_aug)
    state = run_chunk(
        [first_plane, second_blocks(0, low_at), second_blocks(0, high_at)],
        [first_x, low, high],
        *fixed,
        (top, acc),
    )
    state = run_chunk(
        [
            second_blocks(1, low_at),
            second_blocks(3, high_at),
            second_blocks(1, high_at),
            second_blocks(3, low_at),
        ],
        [low_left, high_right, high_left, low_right],
        *fixed,
        state,
    )
    prompt_attended, decoded = run_chunk(
        [first_blocks((1, 2, 3)), second_blocks(2, low_at), second_blocks(2, high_at)],
        [first_y, low_far, high_far],
        *fixed,
        state,
        final=True,
    )
    decoded = lax.ppermute(decoded, "grp", [(0, 1), (1, 0)])
    step_attended = decoded.reshape(1, 2, 1, GROUP * HEAD)
    return prompt_attended, step_attended


def solution(mesh):
    pools, _, heads = mesh.devices.shape
    fine = Mesh(
        mesh.devices.reshape(pools, SIDE, SIDE, SIDE, heads), ("grp", "y", "x", "z", "tp")
    )
    seq = ("y", "x", "z")
    in_specs = (
        P("grp", seq, "tp"),
        P("grp", seq, "tp"),
        P("grp", seq, "tp"),
        P("grp", None, None, "tp"),
        P("grp", None, None, "tp"),
        P("grp", None, None, "tp"),
        P("grp", None),
        P(),
        P(),
    )
    out_specs = (P("grp", seq, "tp"), P("grp", None, seq, "tp"))
    return jax.shard_map(
        per_device, mesh=fine, in_specs=in_specs, out_specs=out_specs, check_vma=False
    )
```

```python
import functools
import math

import jax
import jax.numpy as jnp
from jax import lax
from jax.experimental import pallas as pl
from jax.experimental.pallas import tpu as pltpu
from jax.sharding import Mesh, PartitionSpec as P

HEAD = 128
HALF = 64
GROUP = 8
SIDE = 4
SPAN = GROUP * HALF
PROMPT_ROWS = 2 * SPAN
DECODE_ROWS = 16
NEAR = 16
KEYS = NEAR * 2 * HALF
TILE_BLOCKS = 8
TILE = TILE_BLOCKS * HALF
PART = 256
MESSAGE = 48
OFFSET_LANE = 72
WIDE = GROUP * HEAD + HEAD
NEG = -1e30
SCALE2 = math.log2(math.e) / math.sqrt(HEAD)
VMEM_BYTES = 24 * 1024 * 1024

VMEM = pl.BlockSpec(memory_space=pltpu.VMEM)
SMEM = pl.BlockSpec(memory_space=pltpu.SMEM)
NT = (((1,), (1,)), ((), ()))


def params():
    return pltpu.CompilerParams(vmem_limit_bytes=VMEM_BYTES)


def cost(rows, keys):
    return pl.CostEstimate(
        flops=4 * rows * keys * 256,
        bytes_accessed=keys * 512 + rows * 2048,
        transcendentals=rows * keys,
    )


def scores_of(queries, keys):
    return lax.dot_general(queries, keys, NT, preferred_element_type=jnp.float32)


def back(at, by):
    return (at + SIDE - by) & (SIDE - 1)


def device_of(y, x, z):
    return (y * SIDE + x) * SIDE + z


def seq_position():
    return lax.axis_index("y"), lax.axis_index("x"), lax.axis_index("z")


def pack_kernel(queries, keys, values, lengths, message, rows):
    y, x, z = seq_position()
    rows[...] = jnp.zeros_like(rows)
    lane = lax.broadcasted_iota(jnp.int32, (1, HEAD), 1)
    for by in range(SIDE):
        mine = device_of(back(y, by), x, z)
        top = by * MESSAGE
        for step in range(2):
            block = queries[0, step].astype(jnp.float32)
            here = lax.broadcasted_iota(jnp.int32, block.shape, 0) == mine
            line = jnp.sum(jnp.where(here, block, 0.0), axis=0, keepdims=True)
            for head in range(GROUP):
                at = top + step * GROUP + head
                rows[at : at + 1, :] = line[:, head * HEAD : (head + 1) * HEAD]
            for source, first in ((keys, 16), (values, 32)):
                block = source[0, step].astype(jnp.float32)
                here = lax.broadcasted_iota(jnp.int32, block.shape, 0) == mine
                at = top + first + step
                rows[at : at + 1, :] = jnp.sum(
                    jnp.where(here, block, 0.0), axis=0, keepdims=True
                )
        length = lengths[0, mine]
        digits = jnp.where(lane == 0, length >> 7, jnp.where(lane == 1, length & 127, 0))
        rows[top + 47 : top + 48, :] = digits.astype(jnp.float32)
    message[...] = rows[...].astype(jnp.bfloat16)


def prepare_kernel(order, message, owners, entry_bias, d_aug, d_acc, rank, reach, table):
    y, x, z = seq_position()
    pool = lax.axis_index("grp")
    places = 2 * SIDE * NEAR
    for place in range(places):
        table[place] = 0
    spots = [order[pool, 2 * NEAR * y + block] for block in range(2 * NEAR)]
    for spot in spots:
        table[spot] = 1
    below = jnp.int32(0)
    for place in range(places):
        taken = table[place]
        table[place] = below
        below = below + taken
    for block in range(2 * NEAR):
        rank[block] = table[spots[block]]
    for by in range(SIDE):
        for half in range(2):
            limit = order[pool, 2 * device_of(back(y, by), x, z) + half]
            reach[2 * by + half] = table[limit]

    lane16 = lax.broadcasted_iota(jnp.int32, (DECODE_ROWS, HEAD), 1)
    last = lax.broadcasted_iota(jnp.int32, (DECODE_ROWS, HEAD), 0) == 15
    step = lax.broadcasted_iota(jnp.int32, (16, 16), 0) >> 3
    known = lax.broadcasted_iota(jnp.int32, (16, 16), 1) <= step
    digit_worth = jnp.where(lane16 == 0, 128.0, jnp.where(lane16 == 1, 1.0, 0.0))
    page = lax.broadcasted_iota(jnp.int32, (64, 64), 0) * 64 + lax.broadcasted_iota(
        jnp.int32, (64, 64), 1
    )
    rank_key = owners[...] * 4096 + page
    packed_key = jnp.concatenate([rank_key[0:32], rank_key[32:64]], axis=1)
    token = lax.broadcasted_iota(jnp.int32, (2 * HALF, 64), 0)
    of_page = lax.broadcasted_iota(jnp.int32, (2 * HALF, 64), 1)
    spread = [
        jnp.where(token == 2 * of_page + odd, 1.0, 0.0).astype(jnp.bfloat16) for odd in range(2)
    ]
    device = lax.broadcasted_iota(jnp.int32, (64, HEAD), 0)
    lane = lax.broadcasted_iota(jnp.int32, (64, HEAD), 1)
    wanted, excess = [], []
    for by in range(SIDE):
        top = by * MESSAGE
        rows = slice(by * DECODE_ROWS, (by + 1) * DECODE_ROWS)
        d_aug[rows, 0:HEAD] = message[top : top + 16, :]
        fresh = scores_of(message[top : top + 16, :], message[top + 16 : top + 32, :])
        fresh = jnp.where(known, fresh, NEG)
        offset = jnp.max(fresh, axis=1, keepdims=True).astype(jnp.bfloat16).astype(jnp.float32)
        d_aug[rows, HEAD : 2 * HEAD] = jnp.where(
            (lane16 >> 4) == by, 1.0, jnp.where(lane16 == OFFSET_LANE, offset, 0.0)
        ).astype(jnp.bfloat16)
        if by == 0:
            weights = jnp.exp2((fresh - offset) * SCALE2)
            d_acc[rows, 0:HEAD] = jnp.dot(
                weights.astype(jnp.bfloat16),
                message[top + 32 : top + 48, :],
                preferred_element_type=jnp.float32,
            )
            d_acc[rows, HEAD : 2 * HEAD] = jnp.broadcast_to(
                jnp.sum(weights, axis=1, keepdims=True), (DECODE_ROWS, HEAD)
            )
        else:
            d_acc[rows, :] = jnp.zeros((DECODE_ROWS, 2 * HEAD), jnp.float32)
        digits = message[top + 32 : top + 48, :].astype(jnp.float32)
        length = jnp.sum(jnp.where(last, digits * digit_worth, 0.0), axis=(0, 1), keepdims=True)
        length = length.astype(jnp.int32)
        wanted.append((length >> 1).astype(jnp.float32))
        excess.append(length & 1)
    bound = [jnp.zeros((1, 1), jnp.int32) for _ in wanted]
    for bit in range(18, -1, -1):
        for by in range(SIDE):
            trial = bound[by] + (1 << bit)
            under = jnp.sum(jnp.where(packed_key < trial, 1.0, 0.0), axis=(0, 1), keepdims=True)
            bound[by] = jnp.where(under <= wanted[by], trial, bound[by])
    read = jnp.zeros((2 * HALF, HEAD), jnp.float32)
    for by in range(SIDE):
        allowed = jnp.zeros((2 * HALF, 64), jnp.float32)
        for odd, limit in ((0, bound[by] + excess[by]), (1, bound[by])):
            some = jnp.where(rank_key < limit, 1.0, 0.0).astype(jnp.bfloat16)
            allowed += scores_of(spread[odd], some)
        place = jnp.where(
            ((lane >> 4) == by) & (device == NEAR * y + (lane & 15)), 1.0, 0.0
        ).astype(jnp.bfloat16)
        read += jnp.dot(allowed.astype(jnp.bfloat16), place, preferred_element_type=jnp.float32)
    lanes = lax.broadcasted_iota(jnp.int32, (2 * HALF, HEAD), 1)
    entry_bias[...] = jnp.where(lanes < 64, (1.0 - read) * NEG, 0.0)


def raise_offsets(q_aug, acc, peak, count):
    part = min(count, PART)
    for first in range(0, count, part):
        rows = slice(first, first + part)
        lane = lax.broadcasted_iota(jnp.int32, (part, HEAD), 1)
        tags = q_aug[rows, HEAD : 2 * HEAD].astype(jnp.float32)
        old = jnp.sum(jnp.where(lane == OFFSET_LANE, tags, 0.0), axis=1, keepdims=True)
        offset = (old + peak[rows, :]).astype(jnp.bfloat16).astype(jnp.float32)
        shrink = jnp.exp2((old - offset) * SCALE2)
        q_aug[rows, HEAD : 2 * HEAD] = jnp.where(lane == OFFSET_LANE, offset, tags).astype(
            jnp.bfloat16
        )
        acc[rows, 0:HEAD] = acc[rows, 0:HEAD] * shrink
        acc[rows, HEAD : 2 * HEAD] = acc[rows, HEAD : 2 * HEAD] * shrink


def attend(q_aug, acc, k_aug, v_aug, peak, rows, tile):
    keys = pl.ds(tile * TILE if isinstance(tile, int) else pl.multiple_of(tile * TILE, TILE), TILE)
    scores = scores_of(q_aug[rows, :], k_aug[keys, :])
    if peak is not None:
        peak[rows, :] = jnp.maximum(peak[rows, :], jnp.max(scores, axis=1, keepdims=True))
    else:
        weights = jnp.exp2(scores * SCALE2).astype(jnp.bfloat16)
        acc[rows, :] += jnp.dot(weights, v_aug[keys, :], preferred_element_type=jnp.float32)


def outgrown(acc):
    return jnp.max(jnp.where(acc[:, HEAD : 2 * HEAD] < 1e30, 0.0, 1.0)) > 0.5


def sweep_prompt(q_aug, acc, k_aug, v_aug, peak, begin, ends):
    near_end = jnp.maximum(jnp.minimum(ends[0], ends[1]), begin)
    far_end = jnp.maximum(ends[0], ends[1])
    longer = jnp.where(ends[1] > ends[0], SPAN, 0)

    def both(tile, carry):
        for first in range(0, PROMPT_ROWS, PART):
            attend(q_aug, acc, k_aug, v_aug, peak, pl.ds(first, PART), tile)
        return carry

    def one(tile, carry):
        for first in range(0, SPAN, PART):
            rows = pl.ds(pl.multiple_of(longer + first, PART), PART)
            attend(q_aug, acc, k_aug, v_aug, peak, rows, tile)
        return carry

    lax.fori_loop(begin, near_end, both, 0)
    lax.fori_loop(near_end, far_end, one, 0)


def assemble_kernel(
    rank, reach, entry_bias, d_in, d_base, plane, k_aug, v_aug, d_out, d_aug, d_acc, peak
):
    lane = lax.broadcasted_iota(jnp.int32, (HALF, HEAD), 1)
    row = lax.broadcasted_iota(jnp.int32, (1, HEAD), 1)
    ones = jnp.ones((HALF, HEAD), jnp.bfloat16)
    for at_x in range(SIDE):
        for at_z in range(SIDE):
            j = at_x * SIDE + at_z
            for half in range(2):
                slot = rank[2 * j + half]
                base = jnp.where(row == OFFSET_LANE, -1.0, 0.0)
                for number in range(2 * SIDE):
                    blocked = jnp.where(slot < reach[number], 0.0, NEG)
                    base = jnp.where(row == 64 + number, blocked, base)
                tokens = slice(half * HALF, (half + 1) * HALF)
                mask = jnp.where(
                    ((lane & 15) == j) & (lane < 64), entry_bias[tokens, :], base
                )
                at = pl.ds(pl.multiple_of(slot * HALF, HALF), HALF)
                k_aug[at, 0:HEAD] = plane[at_x, at_z, tokens, 0:HEAD]
                k_aug[at, HEAD : 2 * HEAD] = mask.astype(jnp.bfloat16)
                v_aug[at, 0:HEAD] = plane[at_x, at_z, tokens, HEAD : 2 * HEAD]
                v_aug[at, HEAD : 2 * HEAD] = ones
    d_aug[...] = d_in[...]
    d_acc[...] = d_base[...]
    rows = SIDE * DECODE_ROWS

    def sweep(peak):
        for tile in range(KEYS // TILE):
            attend(d_aug, d_acc, k_aug, v_aug, peak, slice(0, rows), tile)

    sweep(None)

    @pl.when(outgrown(d_acc))
    def _():
        peak[...] = jnp.zeros_like(peak)
        sweep(peak)
        d_acc[...] = d_base[...]
        raise_offsets(d_aug, d_acc, peak, rows)
        sweep(None)

    total = d_acc[:, HEAD : 2 * HEAD]
    tags = d_aug[:, HEAD : 2 * HEAD].astype(jnp.float32)
    wide = lax.broadcasted_iota(jnp.int32, (rows, HEAD), 1)
    offset = jnp.sum(jnp.where(wide == OFFSET_LANE, tags, 0.0), axis=1, keepdims=True)
    d_out[:, 0:HEAD] = d_acc[:, 0:HEAD] / jnp.maximum(total, 1e-30)
    high = total.astype(jnp.bfloat16).astype(jnp.float32)
    d_out[:, HEAD : 2 * HEAD] = jnp.where(
        wide == 0,
        high,
        jnp.where(wide == 32, total - high, jnp.where(wide == 64, offset, 0.0)),
    )


def group_kernel(by, reach, queries, k_aug, v_aug, d_out, *refs):
    if by == 0:
        own_kv, answer, q_aug, acc, peak, base = refs
    else:
        answer, q_aug, acc, peak = refs
    source = 0 if by == 0 else back(lax.axis_index("y"), by)
    reached = [reach[2 * by + block] for block in range(2)]
    ends = [(count + TILE_BLOCKS - 1) // TILE_BLOCKS for count in reached]
    for block in range(2):
        tokens = slice(block * HALF, (block + 1) * HALF)
        rows = slice(block * SPAN, (block + 1) * SPAN)
        for head in range(GROUP):
            at = block * SPAN + head * HALF
            q_aug[at : at + HALF, 0:HEAD] = queries[
                source, tokens, head * HEAD : (head + 1) * HEAD
            ]
        lane = lax.broadcasted_iota(jnp.int32, (PART, HEAD), 1)
        flag = jnp.where(lane == 64 + 2 * by + block, 1.0, 0.0)
        q_aug[rows, HEAD : 2 * HEAD] = jnp.concatenate([flag] * (SPAN // PART)).astype(
            jnp.bfloat16
        )
    for first in range(0, PROMPT_ROWS, PART):
        block = first // SPAN
        some = slice(first, first + PART)
        flag = jnp.where(lane == 64 + 2 * by + block, 1.0, 0.0)
        if by == 0:
            tokens = slice(block * HALF, (block + 1) * HALF)
            token = lax.broadcasted_iota(jnp.int32, (PART, HALF), 0) & (HALF - 1)
            column = lax.broadcasted_iota(jnp.int32, (PART, HALF), 1)
            scores = scores_of(q_aug[some, 0:HEAD], own_kv[tokens, 0:HEAD])
            scores = jnp.where(column <= token, scores, NEG)
            offset = jnp.max(scores, axis=1, keepdims=True).astype(jnp.bfloat16)
            offset = offset.astype(jnp.float32)
            weights = jnp.exp2((scores - offset) * SCALE2)
            left = jnp.dot(
                weights.astype(jnp.bfloat16),
                own_kv[tokens, HEAD : 2 * HEAD],
                preferred_element_type=jnp.float32,
            )
            right = jnp.broadcast_to(jnp.sum(weights, axis=1, keepdims=True), (PART, HEAD))
            for ref in (acc, base):
                ref[some, 0:HEAD] = left
                ref[some, HEAD : 2 * HEAD] = right
        else:
            scores = scores_of(q_aug[some, :], k_aug[0:TILE, :])
            offset = jnp.max(scores, axis=1, keepdims=True).astype(jnp.bfloat16)
            offset = offset.astype(jnp.float32)
            weights = jnp.exp2((scores - offset) * SCALE2).astype(jnp.bfloat16)
            acc[some, :] = jnp.dot(
                weights, v_aug[0:TILE, :], preferred_element_type=jnp.float32
            ) * jnp.where(reached[block] > 0, 1.0, 0.0)
        q_aug[some, HEAD : 2 * HEAD] = jnp.where(lane == OFFSET_LANE, offset, flag).astype(
            jnp.bfloat16
        )

    sweep_prompt(q_aug, acc, k_aug, v_aug, None, 0 if by == 0 else 1, ends)

    @pl.when(outgrown(acc))
    def _():
        peak[...] = jnp.zeros_like(peak)
        sweep_prompt(q_aug, acc, k_aug, v_aug, peak, 0, ends)
        acc[...] = base[...] if by == 0 else jnp.zeros_like(acc)
        raise_offsets(q_aug, acc, peak, PROMPT_ROWS)
        sweep_prompt(q_aug, acc, k_aug, v_aug, None, 0, ends)

    wide = lax.broadcasted_iota(jnp.int32, (HALF, HEAD), 1)
    for block in range(2):
        tokens = slice(block * HALF, (block + 1) * HALF)
        extra = jnp.zeros((HALF, HEAD), jnp.float32)
        for head in range(GROUP):
            at = block * SPAN + head * HALF
            rows = slice(at, at + HALF)
            total = acc[rows, HEAD : 2 * HEAD]
            tags = q_aug[rows, HEAD : 2 * HEAD].astype(jnp.float32)
            offset = jnp.sum(jnp.where(wide == OFFSET_LANE, tags, 0.0), axis=1, keepdims=True)
            high = total.astype(jnp.bfloat16).astype(jnp.float32)
            extra = jnp.where(wide == head, high, extra)
            extra = jnp.where(wide == 32 + head, total - high, extra)
            extra = jnp.where(wide == 64 + head, offset, extra)
            answer[tokens, head * HEAD : (head + 1) * HEAD] = (
                acc[rows, 0:HEAD] / jnp.maximum(total, 1e-30)
            ).astype(answer.dtype)
        answer[tokens, GROUP * HEAD : WIDE] = extra.astype(answer.dtype)
    decoded = slice(2 * HALF, 2 * HALF + DECODE_ROWS)
    mine = slice(by * DECODE_ROWS, (by + 1) * DECODE_ROWS)
    answer[decoded, 0 : 2 * HEAD] = d_out[mine, :].astype(answer.dtype)
    answer[decoded, 2 * HEAD : WIDE] = jnp.zeros(
        (DECODE_ROWS, WIDE - 2 * HEAD), answer.dtype
    )


def merge_kernel(*refs):
    answers, (prompt_out, decode_out) = refs[:SIDE], refs[SIDE:]

    def shares(extras):
        extras = [extra.astype(jnp.float32) for extra in extras]
        totals = [extra + pltpu.roll(extra, HEAD - 32, 1) for extra in extras]
        offsets = [pltpu.roll(extra, HEAD - 64, 1) for extra in extras]
        top = functools.reduce(jnp.maximum, offsets)
        parts = [
            total * jnp.exp2((offset - top) * SCALE2) for total, offset in zip(totals, offsets)
        ]
        whole = functools.reduce(jnp.add, parts)
        return [part / whole for part in parts]

    for block in range(2):
        tokens = slice(block * HALF, (block + 1) * HALF)
        parts = shares([answer[tokens, GROUP * HEAD : WIDE] for answer in answers])
        for head in range(GROUP):
            lanes = slice(head * HEAD, (head + 1) * HEAD)
            prompt_out[0, tokens, lanes] = functools.reduce(
                jnp.add,
                [
                    answer[tokens, lanes].astype(jnp.float32) * part[:, head : head + 1]
                    for answer, part in zip(answers, parts)
                ],
            ).astype(jnp.bfloat16)
    rows = slice(2 * HALF, 2 * HALF + DECODE_ROWS)
    parts = shares([answer[rows, HEAD : 2 * HEAD] for answer in answers])
    decode_out[...] = functools.reduce(
        jnp.add,
        [
            answer[rows, 0:HEAD].astype(jnp.float32) * part[:, 0:1]
            for answer, part in zip(answers, parts)
        ],
    ).astype(jnp.bfloat16)


def rotate(block, axis, by):
    return lax.ppermute(block, axis, [(i, (i + by) % SIDE) for i in range(SIDE)])


def gather_all(block, axis):
    copies = jnp.broadcast_to(block[None], (SIDE,) + block.shape)
    return lax.all_to_all(copies, axis, split_axis=0, concat_axis=0, tiled=True)


def per_device(
    prompt_queries,
    prompt_keys,
    prefill_value_rows,
    step_queries,
    step_keys,
    decode_step_values,
    context_lengths,
    span_order,
    page_owner,
):
    own_kv = jnp.concatenate([prompt_keys[0], prefill_value_rows[0]], axis=1)
    z_line = gather_all(own_kv, "z")
    all_queries = gather_all(prompt_queries[0], "y")
    plane = gather_all(z_line, "x")

    message = pl.pallas_call(
        pack_kernel,
        out_shape=jax.ShapeDtypeStruct((SIDE * MESSAGE, HEAD), jnp.bfloat16),
        in_specs=[VMEM, VMEM, VMEM, SMEM],
        out_specs=VMEM,
        scratch_shapes=[pltpu.VMEM((SIDE * MESSAGE, HEAD), jnp.float32)],
        compiler_params=params(),
    )(step_queries, step_keys, decode_step_values, context_lengths)
    message = lax.ppermute(message, "grp", [(0, 1), (1, 0)])
    pool = lax.axis_index("grp")
    owners = lax.dynamic_index_in_dim(page_owner, pool, 0, keepdims=False).reshape(64, 64)
    rows = SIDE * DECODE_ROWS
    entry_bias, d_aug, d_acc, rank, reach = pl.pallas_call(
        prepare_kernel,
        out_shape=[
            jax.ShapeDtypeStruct((2 * HALF, HEAD), jnp.float32),
            jax.ShapeDtypeStruct((rows, 2 * HEAD), jnp.bfloat16),
            jax.ShapeDtypeStruct((rows, 2 * HEAD), jnp.float32),
            jax.ShapeDtypeStruct((2 * NEAR,), jnp.int32),
            jax.ShapeDtypeStruct((2 * SIDE,), jnp.int32),
        ],
        in_specs=[SMEM, VMEM, VMEM],
        out_specs=[VMEM, VMEM, VMEM, SMEM, SMEM],
        scratch_shapes=[pltpu.SMEM((2 * SIDE * NEAR,), jnp.int32)],
        compiler_params=params(),
        cost_estimate=cost(1024, 512),
    )(span_order, message, owners)
    k_aug, v_aug, d_out = pl.pallas_call(
        assemble_kernel,
        out_shape=[
            jax.ShapeDtypeStruct((KEYS, 2 * HEAD), jnp.bfloat16),
            jax.ShapeDtypeStruct((KEYS, 2 * HEAD), jnp.bfloat16),
            jax.ShapeDtypeStruct((rows, 2 * HEAD), jnp.float32),
        ],
        in_specs=[SMEM, SMEM] + [VMEM] * 4,
        out_specs=[VMEM] * 3,
        scratch_shapes=[
            pltpu.VMEM((rows, 2 * HEAD), jnp.bfloat16),
            pltpu.VMEM((rows, 2 * HEAD), jnp.float32),
            pltpu.VMEM((rows, HEAD), jnp.float32),
        ],
        compiler_params=params(),
        cost_estimate=cost(256, KEYS),
    )(rank, reach, entry_bias, d_aug, d_acc, plane)

    answers = {}
    for by in (2, 1, 3, 0):
        own = [own_kv] if by == 0 else []
        kind = jnp.float32 if by == 0 else jnp.bfloat16
        answer = pl.pallas_call(
            functools.partial(group_kernel, by),
            out_shape=jax.ShapeDtypeStruct((2 * HALF + DECODE_ROWS, WIDE), kind),
            in_specs=[SMEM] + [VMEM] * (4 + len(own)),
            out_specs=VMEM,
            scratch_shapes=[
                pltpu.VMEM((PROMPT_ROWS, 2 * HEAD), jnp.bfloat16),
                pltpu.VMEM((PROMPT_ROWS, 2 * HEAD), jnp.float32),
                pltpu.VMEM((PROMPT_ROWS, HEAD), jnp.float32),
            ]
            + [pltpu.VMEM((PROMPT_ROWS, 2 * HEAD), jnp.float32)] * len(own),
            compiler_params=params(),
            cost_estimate=cost(PROMPT_ROWS, KEYS),
        )(reach, prompt_queries if by == 0 else all_queries, k_aug, v_aug, d_out, *own)
        answers[by] = answer if by == 0 else rotate(answer, "y", SIDE - by)
    prompt_attended, decoded = pl.pallas_call(
        merge_kernel,
        out_shape=[
            jax.ShapeDtypeStruct((1, 2 * HALF, GROUP * HEAD), jnp.bfloat16),
            jax.ShapeDtypeStruct((DECODE_ROWS, HEAD), jnp.bfloat16),
        ],
        in_specs=[VMEM] * SIDE,
        out_specs=[VMEM] * 2,
        compiler_params=params(),
        cost_estimate=cost(128, 512),
    )(*[answers[by] for by in range(SIDE)])
    decoded = lax.ppermute(decoded, "grp", [(0, 1), (1, 0)])
    step_attended = decoded.reshape(1, 2, 1, GROUP * HEAD)
    return prompt_attended, step_attended


def solution(mesh):
    pools, _, heads = mesh.devices.shape
    fine = Mesh(
        mesh.devices.reshape(pools, SIDE, SIDE, SIDE, heads), ("grp", "y", "x", "z", "tp")
    )
    seq = ("y", "x", "z")
    in_specs = (
        P("grp", seq, "tp"),
        P("grp", seq, "tp"),
        P("grp", seq, "tp"),
        P("grp", None, None, "tp"),
        P("grp", None, None, "tp"),
        P("grp", None, None, "tp"),
        P("grp", None),
        P(),
        P(),
    )
    out_specs = (P("grp", seq, "tp"), P("grp", None, seq, "tp"))
    return jax.shard_map(
        per_device, mesh=fine, in_specs=in_specs, out_specs=out_specs, check_vma=False
    )
```

```python
import functools
import math

import jax
import jax.numpy as jnp
from jax import lax
from jax.experimental import pallas as pl
from jax.experimental.pallas import tpu as pltpu
from jax.sharding import Mesh, PartitionSpec as P

HEAD = 128
HALF = 64
GROUP = 8
SIDE = 4
SPAN = GROUP * HALF
PROMPT_ROWS = 2 * SPAN
DECODE_ROWS = 16
NEAR = 16
KEYS = NEAR * 2 * HALF
TILE_BLOCKS = 8
TILE = TILE_BLOCKS * HALF
PART = 256
MESSAGE = 48
OFFSET_LANE = 72
WIDE = GROUP * HEAD + HEAD
NEG = -1e30
SCALE2 = math.log2(math.e) / math.sqrt(HEAD)
VMEM_BYTES = 24 * 1024 * 1024

VMEM = pl.BlockSpec(memory_space=pltpu.VMEM)
SMEM = pl.BlockSpec(memory_space=pltpu.SMEM)
NT = (((1,), (1,)), ((), ()))


def params():
    return pltpu.CompilerParams(vmem_limit_bytes=VMEM_BYTES)


def cost(rows, keys):
    return pl.CostEstimate(
        flops=4 * rows * keys * 256,
        bytes_accessed=keys * 512 + rows * 2048,
        transcendentals=rows * keys,
    )


def scores_of(queries, keys):
    return lax.dot_general(queries, keys, NT, preferred_element_type=jnp.float32)


def back(at, by):
    return (at + SIDE - by) & (SIDE - 1)


def device_of(y, x, z):
    return (y * SIDE + x) * SIDE + z


def seq_position():
    return lax.axis_index("y"), lax.axis_index("x"), lax.axis_index("z")


def pack_kernel(queries, keys, values, lengths, message, rows):
    y, x, z = seq_position()
    rows[...] = jnp.zeros_like(rows)
    lane = lax.broadcasted_iota(jnp.int32, (1, HEAD), 1)
    for by in range(SIDE):
        mine = device_of(back(y, by), x, z)
        top = by * MESSAGE
        for step in range(2):
            block = queries[0, step].astype(jnp.float32)
            here = lax.broadcasted_iota(jnp.int32, block.shape, 0) == mine
            line = jnp.sum(jnp.where(here, block, 0.0), axis=0, keepdims=True)
            for head in range(GROUP):
                at = top + step * GROUP + head
                rows[at : at + 1, :] = line[:, head * HEAD : (head + 1) * HEAD]
            for source, first in ((keys, 16), (values, 32)):
                block = source[0, step].astype(jnp.float32)
                here = lax.broadcasted_iota(jnp.int32, block.shape, 0) == mine
                at = top + first + step
                rows[at : at + 1, :] = jnp.sum(
                    jnp.where(here, block, 0.0), axis=0, keepdims=True
                )
        length = lengths[0, mine]
        digits = jnp.where(lane == 0, length >> 7, jnp.where(lane == 1, length & 127, 0))
        rows[top + 47 : top + 48, :] = digits.astype(jnp.float32)
    message[...] = rows[...].astype(jnp.bfloat16)


def prepare_kernel(order, message, owners, entry_bias, d_aug, d_acc, rank, reach, table):
    y, x, z = seq_position()
    pool = lax.axis_index("grp")
    places = 2 * SIDE * NEAR
    for place in range(places):
        table[place] = 0
    spots = [order[pool, 2 * NEAR * y + block] for block in range(2 * NEAR)]
    for spot in spots:
        table[spot] = 1
    below = jnp.int32(0)
    for place in range(places):
        taken = table[place]
        table[place] = below
        below = below + taken
    for block in range(2 * NEAR):
        rank[block] = table[spots[block]]
    for by in range(SIDE):
        for half in range(2):
            limit = order[pool, 2 * device_of(back(y, by), x, z) + half]
            reach[2 * by + half] = table[limit]

    lane16 = lax.broadcasted_iota(jnp.int32, (DECODE_ROWS, HEAD), 1)
    last = lax.broadcasted_iota(jnp.int32, (DECODE_ROWS, HEAD), 0) == 15
    step = lax.broadcasted_iota(jnp.int32, (16, 16), 0) >> 3
    known = lax.broadcasted_iota(jnp.int32, (16, 16), 1) <= step
    digit_worth = jnp.where(lane16 == 0, 128.0, jnp.where(lane16 == 1, 1.0, 0.0))
    page = lax.broadcasted_iota(jnp.int32, (64, 64), 0) * 64 + lax.broadcasted_iota(
        jnp.int32, (64, 64), 1
    )
    rank_key = owners[...] * 4096 + page
    packed_key = jnp.concatenate([rank_key[0:32], rank_key[32:64]], axis=1)
    token = lax.broadcasted_iota(jnp.int32, (2 * HALF, 64), 0)
    of_page = lax.broadcasted_iota(jnp.int32, (2 * HALF, 64), 1)
    spread = [
        jnp.where(token == 2 * of_page + odd, 1.0, 0.0).astype(jnp.bfloat16) for odd in range(2)
    ]
    device = lax.broadcasted_iota(jnp.int32, (64, HEAD), 0)
    lane = lax.broadcasted_iota(jnp.int32, (64, HEAD), 1)
    wanted, excess = [], []
    for by in range(SIDE):
        top = by * MESSAGE
        rows = slice(by * DECODE_ROWS, (by + 1) * DECODE_ROWS)
        d_aug[rows, 0:HEAD] = message[top : top + 16, :]
        fresh = scores_of(message[top : top + 16, :], message[top + 16 : top + 32, :])
        fresh = jnp.where(known, fresh, NEG)
        offset = jnp.max(fresh, axis=1, keepdims=True).astype(jnp.bfloat16).astype(jnp.float32)
        d_aug[rows, HEAD : 2 * HEAD] = jnp.where(
            (lane16 >> 4) == by, 1.0, jnp.where(lane16 == OFFSET_LANE, offset, 0.0)
        ).astype(jnp.bfloat16)
        if by == 0:
            weights = jnp.exp2((fresh - offset) * SCALE2)
            d_acc[rows, 0:HEAD] = jnp.dot(
                weights.astype(jnp.bfloat16),
                message[top + 32 : top + 48, :],
                preferred_element_type=jnp.float32,
            )
            d_acc[rows, HEAD : 2 * HEAD] = jnp.broadcast_to(
                jnp.sum(weights, axis=1, keepdims=True), (DECODE_ROWS, HEAD)
            )
        else:
            d_acc[rows, :] = jnp.zeros((DECODE_ROWS, 2 * HEAD), jnp.float32)
        digits = message[top + 32 : top + 48, :].astype(jnp.float32)
        length = jnp.sum(jnp.where(last, digits * digit_worth, 0.0), axis=(0, 1), keepdims=True)
        length = length.astype(jnp.int32)
        wanted.append((length >> 1).astype(jnp.float32))
        excess.append(length & 1)
    bound = [jnp.zeros((1, 1), jnp.int32) for _ in wanted]
    for bit in range(18, -1, -1):
        for by in range(SIDE):
            trial = bound[by] + (1 << bit)
            under = jnp.sum(jnp.where(packed_key < trial, 1.0, 0.0), axis=(0, 1), keepdims=True)
            bound[by] = jnp.where(under <= wanted[by], trial, bound[by])
    read = jnp.zeros((2 * HALF, HEAD), jnp.float32)
    for by in range(SIDE):
        allowed = jnp.zeros((2 * HALF, 64), jnp.float32)
        for odd, limit in ((0, bound[by] + excess[by]), (1, bound[by])):
            some = jnp.where(rank_key < limit, 1.0, 0.0).astype(jnp.bfloat16)
            allowed += scores_of(spread[odd], some)
        place = jnp.where(
            ((lane >> 4) == by) & (device == NEAR * y + (lane & 15)), 1.0, 0.0
        ).astype(jnp.bfloat16)
        read += jnp.dot(allowed.astype(jnp.bfloat16), place, preferred_element_type=jnp.float32)
    lanes = lax.broadcasted_iota(jnp.int32, (2 * HALF, HEAD), 1)
    entry_bias[...] = jnp.where(lanes < 64, (1.0 - read) * NEG, 0.0)


def raise_offsets(q_aug, acc, peak, count):
    part = min(count, PART)
    for first in range(0, count, part):
        rows = slice(first, first + part)
        lane = lax.broadcasted_iota(jnp.int32, (part, HEAD), 1)
        tags = q_aug[rows, HEAD : 2 * HEAD].astype(jnp.float32)
        old = jnp.sum(jnp.where(lane == OFFSET_LANE, tags, 0.0), axis=1, keepdims=True)
        offset = (old + peak[rows, :]).astype(jnp.bfloat16).astype(jnp.float32)
        shrink = jnp.exp2((old - offset) * SCALE2)
        q_aug[rows, HEAD : 2 * HEAD] = jnp.where(lane == OFFSET_LANE, offset, tags).astype(
            jnp.bfloat16
        )
        acc[rows, 0:HEAD] = acc[rows, 0:HEAD] * shrink
        acc[rows, HEAD : 2 * HEAD] = acc[rows, HEAD : 2 * HEAD] * shrink


def attend(q_aug, acc, k_turned, v_aug, peak, rows, tile):
    keys = pl.ds(tile * TILE if isinstance(tile, int) else pl.multiple_of(tile * TILE, TILE), TILE)
    scores = jnp.dot(q_aug[rows, :], k_turned[:, keys], preferred_element_type=jnp.float32)
    if peak is not None:
        peak[rows, :] = jnp.maximum(peak[rows, :], jnp.max(scores, axis=1, keepdims=True))
    else:
        weights = jnp.exp2(scores * SCALE2).astype(jnp.bfloat16)
        acc[rows, :] += jnp.dot(weights, v_aug[keys, :], preferred_element_type=jnp.float32)


def outgrown(acc):
    return jnp.max(jnp.where(acc[:, HEAD : 2 * HEAD] < 1e30, 0.0, 1.0)) > 0.5


def sweep_prompt(q_aug, acc, k_turned, v_aug, peak, begin, ends):
    near_end = jnp.maximum(jnp.minimum(ends[0], ends[1]), begin)
    far_end = jnp.maximum(ends[0], ends[1])
    longer = jnp.where(ends[1] > ends[0], SPAN, 0)

    def both(tile, carry):
        for first in range(0, PROMPT_ROWS, SPAN):
            attend(q_aug, acc, k_turned, v_aug, peak, pl.ds(first, SPAN), tile)
        return carry

    def one(tile, carry):
        for first in range(0, SPAN, PART):
            rows = pl.ds(pl.multiple_of(longer + first, PART), PART)
            attend(q_aug, acc, k_turned, v_aug, peak, rows, tile)
        return carry

    lax.fori_loop(begin, near_end, both, 0)
    lax.fori_loop(near_end, far_end, one, 0)


def assemble_kernel(
    rank, reach, entry_bias, d_in, d_base, plane, k_turned, v_aug, d_out, k_aug, d_aug, d_acc, peak
):
    lane = lax.broadcasted_iota(jnp.int32, (HALF, HEAD), 1)
    row = lax.broadcasted_iota(jnp.int32, (1, HEAD), 1)
    ones = jnp.ones((HALF, HEAD), jnp.bfloat16)
    for at_x in range(SIDE):
        for at_z in range(SIDE):
            j = at_x * SIDE + at_z
            for half in range(2):
                slot = rank[2 * j + half]
                base = jnp.where(row == OFFSET_LANE, -1.0, 0.0)
                for number in range(2 * SIDE):
                    blocked = jnp.where(slot < reach[number], 0.0, NEG)
                    base = jnp.where(row == 64 + number, blocked, base)
                tokens = slice(half * HALF, (half + 1) * HALF)
                mask = jnp.where(
                    ((lane & 15) == j) & (lane < 64), entry_bias[tokens, :], base
                )
                at = pl.ds(pl.multiple_of(slot * HALF, HALF), HALF)
                k_aug[at, 0:HEAD] = plane[at_x, at_z, tokens, 0:HEAD]
                k_aug[at, HEAD : 2 * HEAD] = mask.astype(jnp.bfloat16)
                v_aug[at, 0:HEAD] = plane[at_x, at_z, tokens, HEAD : 2 * HEAD]
                v_aug[at, HEAD : 2 * HEAD] = ones
    for first in range(0, KEYS, 2 * HEAD):
        some = slice(first, first + 2 * HEAD)
        k_turned[:, some] = k_aug[some, :].T
    d_aug[...] = d_in[...]
    d_acc[...] = d_base[...]
    rows = SIDE * DECODE_ROWS

    def sweep(peak):
        for tile in range(KEYS // TILE):
            attend(d_aug, d_acc, k_turned, v_aug, peak, slice(0, rows), tile)

    sweep(None)

    @pl.when(outgrown(d_acc))
    def _():
        peak[...] = jnp.zeros_like(peak)
        sweep(peak)
        d_acc[...] = d_base[...]
        raise_offsets(d_aug, d_acc, peak, rows)
        sweep(None)

    total = d_acc[:, HEAD : 2 * HEAD]
    tags = d_aug[:, HEAD : 2 * HEAD].astype(jnp.float32)
    wide = lax.broadcasted_iota(jnp.int32, (rows, HEAD), 1)
    offset = jnp.sum(jnp.where(wide == OFFSET_LANE, tags, 0.0), axis=1, keepdims=True)
    d_out[:, 0:HEAD] = d_acc[:, 0:HEAD] / jnp.maximum(total, 1e-30)
    high = total.astype(jnp.bfloat16).astype(jnp.float32)
    d_out[:, HEAD : 2 * HEAD] = jnp.where(
        wide == 0,
        high,
        jnp.where(wide == 32, total - high, jnp.where(wide == 64, offset, 0.0)),
    )


def group_kernel(by, reach, queries, k_turned, v_aug, d_out, *refs):
    if by == 0:
        own_kv, answer, q_aug, acc, peak, base = refs
    else:
        answer, q_aug, acc, peak = refs
    reached = [reach[2 * by + block] for block in range(2)]
    ends = [(count + TILE_BLOCKS - 1) // TILE_BLOCKS for count in reached]
    for block in range(2):
        tokens = slice(block * HALF, (block + 1) * HALF)
        rows = slice(block * SPAN, (block + 1) * SPAN)
        for head in range(GROUP):
            at = block * SPAN + head * HALF
            q_aug[at : at + HALF, 0:HEAD] = queries[tokens, head * HEAD : (head + 1) * HEAD]
        lane = lax.broadcasted_iota(jnp.int32, (PART, HEAD), 1)
        flag = jnp.where(lane == 64 + 2 * by + block, 1.0, 0.0)
        q_aug[rows, HEAD : 2 * HEAD] = jnp.concatenate([flag] * (SPAN // PART)).astype(
            jnp.bfloat16
        )
    for first in range(0, PROMPT_ROWS, PART):
        block = first // SPAN
        some = slice(first, first + PART)
        flag = jnp.where(lane == 64 + 2 * by + block, 1.0, 0.0)
        if by == 0:
            tokens = slice(block * HALF, (block + 1) * HALF)
            token = lax.broadcasted_iota(jnp.int32, (PART, HALF), 0) & (HALF - 1)
            column = lax.broadcasted_iota(jnp.int32, (PART, HALF), 1)
            scores = scores_of(q_aug[some, 0:HEAD], own_kv[tokens, 0:HEAD])
            scores = jnp.where(column <= token, scores, NEG)
            offset = jnp.max(scores, axis=1, keepdims=True).astype(jnp.bfloat16)
            offset = offset.astype(jnp.float32)
            weights = jnp.exp2((scores - offset) * SCALE2)
            left = jnp.dot(
                weights.astype(jnp.bfloat16),
                own_kv[tokens, HEAD : 2 * HEAD],
                preferred_element_type=jnp.float32,
            )
            right = jnp.broadcast_to(jnp.sum(weights, axis=1, keepdims=True), (PART, HEAD))
            for ref in (acc, base):
                ref[some, 0:HEAD] = left
                ref[some, HEAD : 2 * HEAD] = right
        else:
            scores = jnp.dot(
                q_aug[some, :], k_turned[:, 0:TILE], preferred_element_type=jnp.float32
            )
            offset = jnp.max(scores, axis=1, keepdims=True).astype(jnp.bfloat16)
            offset = offset.astype(jnp.float32)
            weights = jnp.exp2((scores - offset) * SCALE2).astype(jnp.bfloat16)
            acc[some, :] = jnp.dot(
                weights, v_aug[0:TILE, :], preferred_element_type=jnp.float32
            ) * jnp.where(reached[block] > 0, 1.0, 0.0)
        q_aug[some, HEAD : 2 * HEAD] = jnp.where(lane == OFFSET_LANE, offset, flag).astype(
            jnp.bfloat16
        )

    sweep_prompt(q_aug, acc, k_turned, v_aug, None, 0 if by == 0 else 1, ends)

    @pl.when(outgrown(acc))
    def _():
        peak[...] = jnp.zeros_like(peak)
        sweep_prompt(q_aug, acc, k_turned, v_aug, peak, 0, ends)
        acc[...] = base[...] if by == 0 else jnp.zeros_like(acc)
        raise_offsets(q_aug, acc, peak, PROMPT_ROWS)
        sweep_prompt(q_aug, acc, k_turned, v_aug, None, 0, ends)

    wide = lax.broadcasted_iota(jnp.int32, (HALF, HEAD), 1)
    for block in range(2):
        tokens = slice(block * HALF, (block + 1) * HALF)
        extra = jnp.zeros((HALF, HEAD), jnp.float32)
        for head in range(GROUP):
            at = block * SPAN + head * HALF
            rows = slice(at, at + HALF)
            total = acc[rows, HEAD : 2 * HEAD]
            tags = q_aug[rows, HEAD : 2 * HEAD].astype(jnp.float32)
            offset = jnp.sum(jnp.where(wide == OFFSET_LANE, tags, 0.0), axis=1, keepdims=True)
            high = total.astype(jnp.bfloat16).astype(jnp.float32)
            extra = jnp.where(wide == head, high, extra)
            extra = jnp.where(wide == 32 + head, total - high, extra)
            extra = jnp.where(wide == 64 + head, offset, extra)
            answer[tokens, head * HEAD : (head + 1) * HEAD] = (
                acc[rows, 0:HEAD] / jnp.maximum(total, 1e-30)
            ).astype(answer.dtype)
        answer[tokens, GROUP * HEAD : WIDE] = extra.astype(answer.dtype)
    decoded = slice(2 * HALF, 2 * HALF + DECODE_ROWS)
    mine = slice(by * DECODE_ROWS, (by + 1) * DECODE_ROWS)
    answer[decoded, 0 : 2 * HEAD] = d_out[mine, :].astype(answer.dtype)
    answer[decoded, 2 * HEAD : WIDE] = jnp.zeros(
        (DECODE_ROWS, WIDE - 2 * HEAD), answer.dtype
    )


def shares(extras):
    extras = [extra.astype(jnp.float32) for extra in extras]
    totals = [extra + pltpu.roll(extra, HEAD - 32, 1) for extra in extras]
    offsets = [pltpu.roll(extra, HEAD - 64, 1) for extra in extras]
    top = functools.reduce(jnp.maximum, offsets)
    parts = [total * jnp.exp2((offset - top) * SCALE2) for total, offset in zip(totals, offsets)]
    whole = functools.reduce(jnp.add, parts)
    return [part / whole for part in parts]


def merge_decode_kernel(*refs):
    answers, decode_out = refs[:SIDE], refs[SIDE]
    rows = slice(2 * HALF, 2 * HALF + DECODE_ROWS)
    parts = shares([answer[rows, HEAD : 2 * HEAD] for answer in answers])
    merged = functools.reduce(
        jnp.add,
        [
            answer[rows, 0:HEAD].astype(jnp.float32) * part[:, 0:1]
            for answer, part in zip(answers, parts)
        ],
    )
    for head in range(GROUP):
        steps = [merged[at : at + 1] for at in (head, GROUP + head)]
        decode_out[:, head * HEAD : (head + 1) * HEAD] = jnp.concatenate(steps, axis=0).astype(
            jnp.bfloat16
        )


def merge_kernel(*refs):
    answers, prompt_out = refs[:SIDE], refs[SIDE]
    for block in range(2):
        tokens = slice(block * HALF, (block + 1) * HALF)
        parts = shares([answer[tokens, GROUP * HEAD : WIDE] for answer in answers])
        for head in range(GROUP):
            lanes = slice(head * HEAD, (head + 1) * HEAD)
            prompt_out[0, tokens, lanes] = functools.reduce(
                jnp.add,
                [
                    answer[tokens, lanes].astype(jnp.float32) * part[:, head : head + 1]
                    for answer, part in zip(answers, parts)
                ],
            ).astype(jnp.bfloat16)


def rotate(block, axis, by):
    return lax.ppermute(block, axis, [(i, (i + by) % SIDE) for i in range(SIDE)])


def gather_all(block, axis):
    copies = jnp.broadcast_to(block[None], (SIDE,) + block.shape)
    return lax.all_to_all(copies, axis, split_axis=0, concat_axis=0, tiled=True)


def per_device(
    prompt_queries,
    prompt_keys,
    prefill_value_rows,
    step_queries,
    step_keys,
    decode_step_values,
    context_lengths,
    span_order,
    page_owner,
):
    own_kv = jnp.concatenate([prompt_keys[0], prefill_value_rows[0]], axis=1)
    z_line = gather_all(own_kv, "z")
    message = pl.pallas_call(
        pack_kernel,
        out_shape=jax.ShapeDtypeStruct((SIDE * MESSAGE, HEAD), jnp.bfloat16),
        in_specs=[VMEM, VMEM, VMEM, SMEM],
        out_specs=VMEM,
        scratch_shapes=[pltpu.VMEM((SIDE * MESSAGE, HEAD), jnp.float32)],
        compiler_params=params(),
    )(step_queries, step_keys, decode_step_values, context_lengths)
    message = lax.ppermute(message, "grp", [(0, 1), (1, 0)])
    pool = lax.axis_index("grp")
    owners = lax.dynamic_index_in_dim(page_owner, pool, 0, keepdims=False).reshape(64, 64)
    rows = SIDE * DECODE_ROWS
    entry_bias, d_aug, d_acc, rank, reach = pl.pallas_call(
        prepare_kernel,
        out_shape=[
            jax.ShapeDtypeStruct((2 * HALF, HEAD), jnp.float32),
            jax.ShapeDtypeStruct((rows, 2 * HEAD), jnp.bfloat16),
            jax.ShapeDtypeStruct((rows, 2 * HEAD), jnp.float32),
            jax.ShapeDtypeStruct((2 * NEAR,), jnp.int32),
            jax.ShapeDtypeStruct((2 * SIDE,), jnp.int32),
        ],
        in_specs=[SMEM, VMEM, VMEM],
        out_specs=[VMEM, VMEM, VMEM, SMEM, SMEM],
        scratch_shapes=[pltpu.SMEM((2 * SIDE * NEAR,), jnp.int32)],
        compiler_params=params(),
        cost_estimate=cost(1024, 512),
    )(span_order, message, owners)
    z_line, entry_bias, sent_queries = lax.optimization_barrier(
        (z_line, entry_bias, prompt_queries[0])
    )
    queries = {by: rotate(sent_queries, "y", by) for by in (2, 1, 3)}
    queries[0] = prompt_queries[0]
    plane = gather_all(z_line, "x")
    k_turned, v_aug, d_out = pl.pallas_call(
        assemble_kernel,
        out_shape=[
            jax.ShapeDtypeStruct((2 * HEAD, KEYS), jnp.bfloat16),
            jax.ShapeDtypeStruct((KEYS, 2 * HEAD), jnp.bfloat16),
            jax.ShapeDtypeStruct((rows, 2 * HEAD), jnp.float32),
        ],
        in_specs=[SMEM, SMEM] + [VMEM] * 4,
        out_specs=[VMEM] * 3,
        scratch_shapes=[
            pltpu.VMEM((KEYS, 2 * HEAD), jnp.bfloat16),
            pltpu.VMEM((rows, 2 * HEAD), jnp.bfloat16),
            pltpu.VMEM((rows, 2 * HEAD), jnp.float32),
            pltpu.VMEM((rows, HEAD), jnp.float32),
        ],
        compiler_params=params(),
        cost_estimate=cost(256, KEYS),
    )(rank, reach, entry_bias, d_aug, d_acc, plane)

    answers = {}
    for by in (2, 1, 3, 0):
        own = [own_kv] if by == 0 else []
        kind = jnp.float32 if by == 0 else jnp.bfloat16
        answer = pl.pallas_call(
            functools.partial(group_kernel, by),
            out_shape=jax.ShapeDtypeStruct((2 * HALF + DECODE_ROWS, WIDE), kind),
            in_specs=[SMEM] + [VMEM] * (4 + len(own)),
            out_specs=VMEM,
            scratch_shapes=[
                pltpu.VMEM((PROMPT_ROWS, 2 * HEAD), jnp.bfloat16),
                pltpu.VMEM((PROMPT_ROWS, 2 * HEAD), jnp.float32),
                pltpu.VMEM((PROMPT_ROWS, HEAD), jnp.float32),
            ]
            + [pltpu.VMEM((PROMPT_ROWS, 2 * HEAD), jnp.float32)] * len(own),
            compiler_params=params(),
            cost_estimate=cost(PROMPT_ROWS, KEYS),
        )(reach, queries[by], k_turned, v_aug, d_out, *own)
        answers[by] = answer if by == 0 else rotate(answer, "y", SIDE - by)
    partial = [answers[by] for by in range(SIDE)]
    decoded = pl.pallas_call(
        merge_decode_kernel,
        out_shape=jax.ShapeDtypeStruct((2, GROUP * HEAD), jnp.bfloat16),
        in_specs=[VMEM] * SIDE,
        out_specs=VMEM,
        compiler_params=params(),
        cost_estimate=cost(16, 64),
    )(*partial)
    decoded = lax.ppermute(decoded, "grp", [(0, 1), (1, 0)])
    prompt_attended = pl.pallas_call(
        merge_kernel,
        out_shape=jax.ShapeDtypeStruct((1, 2 * HALF, GROUP * HEAD), jnp.bfloat16),
        in_specs=[VMEM] * SIDE,
        out_specs=VMEM,
        compiler_params=params(),
        cost_estimate=cost(128, 512),
    )(*partial)
    step_attended = decoded.reshape(1, 2, 1, GROUP * HEAD)
    return prompt_attended, step_attended


def solution(mesh):
    pools, _, heads = mesh.devices.shape
    fine = Mesh(
        mesh.devices.reshape(pools, SIDE, SIDE, SIDE, heads), ("grp", "y", "x", "z", "tp")
    )
    seq = ("y", "x", "z")
    in_specs = (
        P("grp", seq, "tp"),
        P("grp", seq, "tp"),
        P("grp", seq, "tp"),
        P("grp", None, None, "tp"),
        P("grp", None, None, "tp"),
        P("grp", None, None, "tp"),
        P("grp", None),
        P(),
        P(),
    )
    out_specs = (P("grp", seq, "tp"), P("grp", None, seq, "tp"))
    return jax.shard_map(
        per_device, mesh=fine, in_specs=in_specs, out_specs=out_specs, check_vma=False
    )
```

```python
import functools
import math

import jax
import jax.numpy as jnp
from jax import lax
from jax.experimental import pallas as pl
from jax.experimental.pallas import tpu as pltpu
from jax.sharding import Mesh, PartitionSpec as P

HEAD = 128
HALF = 64
GROUP = 8
SIDE = 4
SPAN = GROUP * HALF
PROMPT_ROWS = 2 * SPAN
DECODE_ROWS = 16
NEAR = 16
KEYS = NEAR * 2 * HALF
TILE_BLOCKS = 8
TILE = TILE_BLOCKS * HALF
PART = 256
MESSAGE = 48
OFFSET_LANE = 72
TURNED_LANE = 8
DECODE_LANE = 96
WIDE = GROUP * HEAD + HEAD
NEG = -1e30
SCALE2 = math.log2(math.e) / math.sqrt(HEAD)
VMEM_BYTES = 24 * 1024 * 1024

VMEM = pl.BlockSpec(memory_space=pltpu.VMEM)
SMEM = pl.BlockSpec(memory_space=pltpu.SMEM)
ANY = pl.BlockSpec(memory_space=pl.ANY)
NT = (((1,), (1,)), ((), ()))


def params():
    return pltpu.CompilerParams(vmem_limit_bytes=VMEM_BYTES)


def cost(rows, keys):
    return pl.CostEstimate(
        flops=4 * rows * keys * 256,
        bytes_accessed=keys * 512 + rows * 2048,
        transcendentals=rows * keys,
    )


def scores_of(queries, keys):
    return lax.dot_general(queries, keys, NT, preferred_element_type=jnp.float32)


def back(at, by):
    return (at + SIDE - by) & (SIDE - 1)


def device_of(y, x, z):
    return (y * SIDE + x) * SIDE + z


def seq_position():
    return lax.axis_index("y"), lax.axis_index("x"), lax.axis_index("z")


def start_and_wait(copies):
    for copy in copies:
        copy.start()
    for copy in copies:
        copy.wait()


def join_kernel(keys, values, own_kv, copies, sems):
    targets = [own_kv] + [copies.at[place] for place in range(SIDE)]
    start_and_wait(
        [
            pltpu.make_async_copy(
                source.at[0],
                target.at[:, pl.ds(side * HEAD, HEAD)],
                sems.at[side, number],
            )
            for number, target in enumerate(targets)
            for side, source in enumerate((keys, values))
        ]
    )


def copy_kernel(block, copies, sems):
    start_and_wait(
        [
            pltpu.make_async_copy(block, copies.at[place], sems.at[place])
            for place in range(SIDE)
        ]
    )


def pack_kernel(queries, keys, values, lengths, message, rows):
    y, x, z = seq_position()
    rows[...] = jnp.zeros_like(rows)
    lane = lax.broadcasted_iota(jnp.int32, (1, HEAD), 1)
    for by in range(SIDE):
        mine = device_of(back(y, by), x, z)
        top = by * MESSAGE
        for step in range(2):
            block = queries[0, step].astype(jnp.float32)
            here = lax.broadcasted_iota(jnp.int32, block.shape, 0) == mine
            line = jnp.sum(jnp.where(here, block, 0.0), axis=0, keepdims=True)
            for head in range(GROUP):
                at = top + step * GROUP + head
                rows[at : at + 1, :] = line[:, head * HEAD : (head + 1) * HEAD]
            for source, first in ((keys, 16), (values, 32)):
                block = source[0, step].astype(jnp.float32)
                here = lax.broadcasted_iota(jnp.int32, block.shape, 0) == mine
                at = top + first + step
                rows[at : at + 1, :] = jnp.sum(
                    jnp.where(here, block, 0.0), axis=0, keepdims=True
                )
        length = lengths[0, mine]
        digits = jnp.where(lane == 0, length >> 7, jnp.where(lane == 1, length & 127, 0))
        rows[top + 47 : top + 48, :] = digits.astype(jnp.float32)
    message[...] = rows[...].astype(jnp.bfloat16)


def prepare_kernel(order, message, owners, entry_bias, d_aug, d_acc, rank, reach, table):
    y, x, z = seq_position()
    pool = lax.axis_index("grp")
    places = 2 * SIDE * NEAR
    for place in range(places):
        table[place] = 0
    spots = [order[pool, 2 * NEAR * y + block] for block in range(2 * NEAR)]
    for spot in spots:
        table[spot] = 1
    below = jnp.int32(0)
    for place in range(places):
        taken = table[place]
        table[place] = below
        below = below + taken
    for block in range(2 * NEAR):
        rank[block] = table[spots[block]]
    for by in range(SIDE):
        for half in range(2):
            limit = order[pool, 2 * device_of(back(y, by), x, z) + half]
            reach[2 * by + half] = table[limit]

    lane16 = lax.broadcasted_iota(jnp.int32, (DECODE_ROWS, HEAD), 1)
    last = lax.broadcasted_iota(jnp.int32, (DECODE_ROWS, HEAD), 0) == 15
    step = lax.broadcasted_iota(jnp.int32, (16, 16), 0) >> 3
    known = lax.broadcasted_iota(jnp.int32, (16, 16), 1) <= step
    digit_worth = jnp.where(lane16 == 0, 128.0, jnp.where(lane16 == 1, 1.0, 0.0))
    page = lax.broadcasted_iota(jnp.int32, (64, 64), 0) * 64 + lax.broadcasted_iota(
        jnp.int32, (64, 64), 1
    )
    rank_key = owners[...] * 4096 + page
    packed_key = jnp.concatenate([rank_key[0:32], rank_key[32:64]], axis=1)
    token = lax.broadcasted_iota(jnp.int32, (2 * HALF, 64), 0)
    of_page = lax.broadcasted_iota(jnp.int32, (2 * HALF, 64), 1)
    spread = [
        jnp.where(token == 2 * of_page + odd, 1.0, 0.0).astype(jnp.bfloat16) for odd in range(2)
    ]
    device = lax.broadcasted_iota(jnp.int32, (64, HEAD), 0)
    lane = lax.broadcasted_iota(jnp.int32, (64, HEAD), 1)
    wanted, excess = [], []
    for by in range(SIDE):
        top = by * MESSAGE
        rows = slice(by * DECODE_ROWS, (by + 1) * DECODE_ROWS)
        d_aug[rows, 0:HEAD] = message[top : top + 16, :]
        fresh = scores_of(message[top : top + 16, :], message[top + 16 : top + 32, :])
        fresh = jnp.where(known, fresh, NEG)
        offset = jnp.max(fresh, axis=1, keepdims=True).astype(jnp.bfloat16).astype(jnp.float32)
        d_aug[rows, HEAD : 2 * HEAD] = jnp.where(
            (lane16 >> 4) == by, 1.0, jnp.where(lane16 == OFFSET_LANE, offset, 0.0)
        ).astype(jnp.bfloat16)
        if by == 0:
            weights = jnp.exp2((fresh - offset) * SCALE2)
            d_acc[rows, 0:HEAD] = jnp.dot(
                weights.astype(jnp.bfloat16),
                message[top + 32 : top + 48, :],
                preferred_element_type=jnp.float32,
            )
            d_acc[rows, HEAD : 2 * HEAD] = jnp.broadcast_to(
                jnp.sum(weights, axis=1, keepdims=True), (DECODE_ROWS, HEAD)
            )
        else:
            d_acc[rows, :] = jnp.zeros((DECODE_ROWS, 2 * HEAD), jnp.float32)
        digits = message[top + 32 : top + 48, :].astype(jnp.float32)
        length = jnp.sum(jnp.where(last, digits * digit_worth, 0.0), axis=(0, 1), keepdims=True)
        length = length.astype(jnp.int32)
        wanted.append((length >> 1).astype(jnp.float32))
        excess.append(length & 1)
    bound = [jnp.zeros((1, 1), jnp.int32) for _ in wanted]
    for bit in range(18, -1, -1):
        for by in range(SIDE):
            trial = bound[by] + (1 << bit)
            under = jnp.sum(jnp.where(packed_key < trial, 1.0, 0.0), axis=(0, 1), keepdims=True)
            bound[by] = jnp.where(under <= wanted[by], trial, bound[by])
    read = jnp.zeros((2 * HALF, HEAD), jnp.float32)
    for by in range(SIDE):
        allowed = jnp.zeros((2 * HALF, 64), jnp.float32)
        for odd, limit in ((0, bound[by] + excess[by]), (1, bound[by])):
            some = jnp.where(rank_key < limit, 1.0, 0.0).astype(jnp.bfloat16)
            allowed += scores_of(spread[odd], some)
        place = jnp.where(
            ((lane >> 4) == by) & (device == NEAR * y + (lane & 15)), 1.0, 0.0
        ).astype(jnp.bfloat16)
        read += jnp.dot(allowed.astype(jnp.bfloat16), place, preferred_element_type=jnp.float32)
    lanes = lax.broadcasted_iota(jnp.int32, (2 * HALF, HEAD), 1)
    entry_bias[...] = jnp.where(lanes < 64, (1.0 - read) * NEG, 0.0)


def raise_offsets(q_aug, acc, peak, count):
    part = min(count, PART)
    for first in range(0, count, part):
        rows = slice(first, first + part)
        lane = lax.broadcasted_iota(jnp.int32, (part, HEAD), 1)
        tags = q_aug[rows, HEAD : 2 * HEAD].astype(jnp.float32)
        old = jnp.sum(jnp.where(lane == OFFSET_LANE, tags, 0.0), axis=1, keepdims=True)
        offset = (old + peak[rows, :]).astype(jnp.bfloat16).astype(jnp.float32)
        shrink = jnp.exp2((old - offset) * SCALE2)
        q_aug[rows, HEAD : 2 * HEAD] = jnp.where(lane == OFFSET_LANE, offset, tags).astype(
            jnp.bfloat16
        )
        acc[rows, 0:HEAD] = acc[rows, 0:HEAD] * shrink
        acc[rows, HEAD : 2 * HEAD] = acc[rows, HEAD : 2 * HEAD] * shrink


def attend(q_aug, acc, k_turned, v_aug, peak, rows, tile):
    keys = pl.ds(tile * TILE if isinstance(tile, int) else pl.multiple_of(tile * TILE, TILE), TILE)
    scores = jnp.dot(q_aug[rows, :], k_turned[:, keys], preferred_element_type=jnp.float32)
    if peak is not None:
        peak[rows, :] = jnp.maximum(peak[rows, :], jnp.max(scores, axis=1, keepdims=True))
    else:
        weights = jnp.exp2(scores * SCALE2).astype(jnp.bfloat16)
        acc[rows, :] += jnp.dot(weights, v_aug[keys, :], preferred_element_type=jnp.float32)


def outgrown(acc):
    return jnp.max(jnp.where(acc[:, HEAD : 2 * HEAD] < 1e30, 0.0, 1.0)) > 0.5


def sweep_prompt(q_aug, acc, k_turned, v_aug, peak, begin, ends):
    near_end = jnp.maximum(jnp.minimum(ends[0], ends[1]), begin)
    far_end = jnp.maximum(ends[0], ends[1])
    longer = jnp.where(ends[1] > ends[0], SPAN, 0)

    def both(tile, carry):
        for first in range(0, PROMPT_ROWS, SPAN):
            attend(q_aug, acc, k_turned, v_aug, peak, pl.ds(first, SPAN), tile)
        return carry

    def one(tile, carry):
        for first in range(0, SPAN, PART):
            rows = pl.ds(pl.multiple_of(longer + first, PART), PART)
            attend(q_aug, acc, k_turned, v_aug, peak, rows, tile)
        return carry

    lax.fori_loop(begin, near_end, both, 0)
    lax.fori_loop(near_end, far_end, one, 0)


def assemble_kernel(
    rank, reach, entry_bias, d_in, d_base, plane, k_turned, v_aug, d_turned, d_extra, k_aug, d_aug, d_acc, peak
):
    lane = lax.broadcasted_iota(jnp.int32, (HALF, HEAD), 1)
    row = lax.broadcasted_iota(jnp.int32, (1, HEAD), 1)
    ones = jnp.ones((HALF, HEAD), jnp.bfloat16)
    for at_x in range(SIDE):
        for at_z in range(SIDE):
            j = at_x * SIDE + at_z
            for half in range(2):
                slot = rank[2 * j + half]
                base = jnp.where(row == OFFSET_LANE, -1.0, 0.0)
                for number in range(2 * SIDE):
                    blocked = jnp.where(slot < reach[number], 0.0, NEG)
                    base = jnp.where(row == 64 + number, blocked, base)
                tokens = slice(half * HALF, (half + 1) * HALF)
                mask = jnp.where(
                    ((lane & 15) == j) & (lane < 64), entry_bias[tokens, :], base
                )
                at = pl.ds(pl.multiple_of(slot * HALF, HALF), HALF)
                k_aug[at, 0:HEAD] = plane[at_x, at_z, tokens, 0:HEAD]
                k_aug[at, HEAD : 2 * HEAD] = mask.astype(jnp.bfloat16)
                v_aug[at, 0:HEAD] = plane[at_x, at_z, tokens, HEAD : 2 * HEAD]
                v_aug[at, HEAD : 2 * HEAD] = ones
    for first in range(0, KEYS, 2 * HEAD):
        some = slice(first, first + 2 * HEAD)
        k_turned[:, some] = k_aug[some, :].T
    d_aug[...] = d_in[...]
    d_acc[...] = d_base[...]
    rows = SIDE * DECODE_ROWS

    def sweep(peak):
        for tile in range(KEYS // TILE):
            attend(d_aug, d_acc, k_turned, v_aug, peak, slice(0, rows), tile)

    sweep(None)

    @pl.when(outgrown(d_acc))
    def _():
        peak[...] = jnp.zeros_like(peak)
        sweep(peak)
        d_acc[...] = d_base[...]
        raise_offsets(d_aug, d_acc, peak, rows)
        sweep(None)

    total = d_acc[:, HEAD : 2 * HEAD]
    tags = d_aug[:, HEAD : 2 * HEAD].astype(jnp.float32)
    wide = lax.broadcasted_iota(jnp.int32, (rows, HEAD), 1)
    offset = jnp.sum(jnp.where(wide == OFFSET_LANE, tags, 0.0), axis=1, keepdims=True)
    answer = d_acc[:, 0:HEAD] / jnp.maximum(total, 1e-30)
    d_turned[...] = jnp.concatenate([answer, jnp.zeros((HEAD - rows, HEAD), jnp.float32)]).T
    high = total.astype(jnp.bfloat16).astype(jnp.float32)
    d_extra[...] = jnp.where(
        wide == DECODE_LANE,
        high,
        jnp.where(
            wide == DECODE_LANE + 1,
            total - high,
            jnp.where(wide == DECODE_LANE + 2, offset, 0.0),
        ),
    )


def group_kernel(by, reach, queries, k_turned, v_aug, d_turned, d_extra, *refs):
    if by == 0:
        own_kv, answer, q_aug, acc, peak, base = refs
    else:
        answer, q_aug, acc, peak = refs
    reached = [reach[2 * by + block] for block in range(2)]
    ends = [(count + TILE_BLOCKS - 1) // TILE_BLOCKS for count in reached]
    for block in range(2):
        tokens = slice(block * HALF, (block + 1) * HALF)
        rows = slice(block * SPAN, (block + 1) * SPAN)
        for head in range(GROUP):
            at = block * SPAN + head * HALF
            q_aug[at : at + HALF, 0:HEAD] = queries[tokens, head * HEAD : (head + 1) * HEAD]
        lane = lax.broadcasted_iota(jnp.int32, (PART, HEAD), 1)
        flag = jnp.where(lane == 64 + 2 * by + block, 1.0, 0.0)
        q_aug[rows, HEAD : 2 * HEAD] = jnp.concatenate([flag] * (SPAN // PART)).astype(
            jnp.bfloat16
        )
    for first in range(0, PROMPT_ROWS, PART):
        block = first // SPAN
        some = slice(first, first + PART)
        flag = jnp.where(lane == 64 + 2 * by + block, 1.0, 0.0)
        if by == 0:
            tokens = slice(block * HALF, (block + 1) * HALF)
            token = lax.broadcasted_iota(jnp.int32, (PART, HALF), 0) & (HALF - 1)
            column = lax.broadcasted_iota(jnp.int32, (PART, HALF), 1)
            scores = scores_of(q_aug[some, 0:HEAD], own_kv[tokens, 0:HEAD])
            scores = jnp.where(column <= token, scores, NEG)
            offset = jnp.max(scores, axis=1, keepdims=True).astype(jnp.bfloat16)
            offset = offset.astype(jnp.float32)
            weights = jnp.exp2((scores - offset) * SCALE2)
            left = jnp.dot(
                weights.astype(jnp.bfloat16),
                own_kv[tokens, HEAD : 2 * HEAD],
                preferred_element_type=jnp.float32,
            )
            right = jnp.broadcast_to(jnp.sum(weights, axis=1, keepdims=True), (PART, HEAD))
            for ref in (acc, base):
                ref[some, 0:HEAD] = left
                ref[some, HEAD : 2 * HEAD] = right
        else:
            scores = jnp.dot(
                q_aug[some, :], k_turned[:, 0:TILE], preferred_element_type=jnp.float32
            )
            offset = jnp.max(scores, axis=1, keepdims=True).astype(jnp.bfloat16)
            offset = offset.astype(jnp.float32)
            weights = jnp.exp2((scores - offset) * SCALE2).astype(jnp.bfloat16)
            acc[some, :] = jnp.dot(
                weights, v_aug[0:TILE, :], preferred_element_type=jnp.float32
            ) * jnp.where(reached[block] > 0, 1.0, 0.0)
        q_aug[some, HEAD : 2 * HEAD] = jnp.where(lane == OFFSET_LANE, offset, flag).astype(
            jnp.bfloat16
        )

    sweep_prompt(q_aug, acc, k_turned, v_aug, None, 0 if by == 0 else 1, ends)

    @pl.when(outgrown(acc))
    def _():
        peak[...] = jnp.zeros_like(peak)
        sweep_prompt(q_aug, acc, k_turned, v_aug, peak, 0, ends)
        acc[...] = base[...] if by == 0 else jnp.zeros_like(acc)
        raise_offsets(q_aug, acc, peak, PROMPT_ROWS)
        sweep_prompt(q_aug, acc, k_turned, v_aug, None, 0, ends)

    wide = lax.broadcasted_iota(jnp.int32, (HALF, HEAD), 1)
    for block in range(2):
        tokens = slice(block * HALF, (block + 1) * HALF)
        turned = pltpu.roll(
            d_turned[tokens, :], (HEAD + TURNED_LANE - DECODE_ROWS * by) % HEAD, 1
        )
        extra = jnp.where(
            (wide >= TURNED_LANE) & (wide < TURNED_LANE + DECODE_ROWS), turned, 0.0
        )
        if block == 0:
            mine = d_extra[by * DECODE_ROWS : (by + 1) * DECODE_ROWS, :]
            rest = jnp.zeros((HALF - DECODE_ROWS, HEAD), jnp.float32)
            extra = extra + jnp.concatenate([mine, rest])
        for head in range(GROUP):
            at = block * SPAN + head * HALF
            rows = slice(at, at + HALF)
            total = acc[rows, HEAD : 2 * HEAD]
            tags = q_aug[rows, HEAD : 2 * HEAD].astype(jnp.float32)
            offset = jnp.sum(jnp.where(wide == OFFSET_LANE, tags, 0.0), axis=1, keepdims=True)
            high = total.astype(jnp.bfloat16).astype(jnp.float32)
            extra = jnp.where(wide == head, high, extra)
            extra = jnp.where(wide == 32 + head, total - high, extra)
            extra = jnp.where(wide == 64 + head, offset, extra)
            answer[tokens, head * HEAD : (head + 1) * HEAD] = (
                acc[rows, 0:HEAD] / jnp.maximum(total, 1e-30)
            ).astype(answer.dtype)
        answer[tokens, GROUP * HEAD : WIDE] = extra.astype(answer.dtype)


def shares(extras):
    extras = [extra.astype(jnp.float32) for extra in extras]
    totals = [extra + pltpu.roll(extra, HEAD - 32, 1) for extra in extras]
    offsets = [pltpu.roll(extra, HEAD - 64, 1) for extra in extras]
    top = functools.reduce(jnp.maximum, offsets)
    parts = [total * jnp.exp2((offset - top) * SCALE2) for total, offset in zip(totals, offsets)]
    whole = functools.reduce(jnp.add, parts)
    return [part / whole for part in parts]


def merge_decode_kernel(*refs):
    answers, decode_out = refs[:SIDE], refs[SIDE]
    columns = [answer[:, GROUP * HEAD : WIDE].astype(jnp.float32) for answer in answers]
    firsts = [column[0:DECODE_ROWS] for column in columns]
    at = DECODE_LANE
    totals = [first[:, at : at + 1] + first[:, at + 1 : at + 2] for first in firsts]
    offsets = [first[:, at + 2 : at + 3] for first in firsts]
    top = functools.reduce(jnp.maximum, offsets)
    parts = [total * jnp.exp2((offset - top) * SCALE2) for total, offset in zip(totals, offsets)]
    whole = functools.reduce(jnp.add, parts)
    merged = functools.reduce(
        jnp.add,
        [
            column.T[TURNED_LANE : TURNED_LANE + DECODE_ROWS] * (part / whole)
            for column, part in zip(columns, parts)
        ],
    )
    for head in range(GROUP):
        steps = [merged[at : at + 1] for at in (head, GROUP + head)]
        decode_out[:, head * HEAD : (head + 1) * HEAD] = jnp.concatenate(steps, axis=0).astype(
            jnp.bfloat16
        )


def merge_kernel(*refs):
    answers, prompt_out = refs[:SIDE], refs[SIDE]
    for block in range(2):
        tokens = slice(block * HALF, (block + 1) * HALF)
        parts = shares([answer[tokens, GROUP * HEAD : WIDE] for answer in answers])
        for head in range(GROUP):
            lanes = slice(head * HEAD, (head + 1) * HEAD)
            prompt_out[0, tokens, lanes] = functools.reduce(
                jnp.add,
                [
                    answer[tokens, lanes].astype(jnp.float32) * part[:, head : head + 1]
                    for answer, part in zip(answers, parts)
                ],
            ).astype(jnp.bfloat16)


def rotate(block, axis, by):
    return lax.ppermute(block, axis, [(i, (i + by) % SIDE) for i in range(SIDE)])


def gather_all(copies, axis):
    return lax.all_to_all(copies, axis, split_axis=0, concat_axis=0, tiled=True)


def per_device(
    prompt_queries,
    prompt_keys,
    prefill_value_rows,
    step_queries,
    step_keys,
    decode_step_values,
    context_lengths,
    span_order,
    page_owner,
):
    own_kv, copies = pl.pallas_call(
        join_kernel,
        out_shape=[
            jax.ShapeDtypeStruct((2 * HALF, 2 * HEAD), jnp.bfloat16),
            jax.ShapeDtypeStruct((SIDE, 2 * HALF, 2 * HEAD), jnp.bfloat16),
        ],
        in_specs=[ANY] * 2,
        out_specs=[VMEM, ANY],
        scratch_shapes=[pltpu.SemaphoreType.DMA((2, SIDE + 1))],
        compiler_params=params(),
    )(prompt_keys, prefill_value_rows)
    z_line = gather_all(copies, "z")
    message = pl.pallas_call(
        pack_kernel,
        out_shape=jax.ShapeDtypeStruct((SIDE * MESSAGE, HEAD), jnp.bfloat16),
        in_specs=[VMEM, VMEM, VMEM, SMEM],
        out_specs=VMEM,
        scratch_shapes=[pltpu.VMEM((SIDE * MESSAGE, HEAD), jnp.float32)],
        compiler_params=params(),
    )(step_queries, step_keys, decode_step_values, context_lengths)
    message = lax.ppermute(message, "grp", [(0, 1), (1, 0)])
    pool = lax.axis_index("grp")
    owners = lax.dynamic_index_in_dim(page_owner, pool, 0, keepdims=False).reshape(64, 64)
    rows = SIDE * DECODE_ROWS
    entry_bias, d_aug, d_acc, rank, reach = pl.pallas_call(
        prepare_kernel,
        out_shape=[
            jax.ShapeDtypeStruct((2 * HALF, HEAD), jnp.float32),
            jax.ShapeDtypeStruct((rows, 2 * HEAD), jnp.bfloat16),
            jax.ShapeDtypeStruct((rows, 2 * HEAD), jnp.float32),
            jax.ShapeDtypeStruct((2 * NEAR,), jnp.int32),
            jax.ShapeDtypeStruct((2 * SIDE,), jnp.int32),
        ],
        in_specs=[SMEM, VMEM, VMEM],
        out_specs=[VMEM, VMEM, VMEM, SMEM, SMEM],
        scratch_shapes=[pltpu.SMEM((2 * SIDE * NEAR,), jnp.int32)],
        compiler_params=params(),
        cost_estimate=cost(1024, 512),
    )(span_order, message, owners)
    z_line, entry_bias, sent_queries = lax.optimization_barrier(
        (z_line, entry_bias, prompt_queries[0])
    )
    queries = {by: rotate(sent_queries, "y", by) for by in (2, 1, 3)}
    queries[0] = prompt_queries[0]
    copies = pl.pallas_call(
        copy_kernel,
        out_shape=jax.ShapeDtypeStruct((SIDE,) + z_line.shape, jnp.bfloat16),
        in_specs=[ANY],
        out_specs=ANY,
        scratch_shapes=[pltpu.SemaphoreType.DMA((SIDE,))],
        compiler_params=params(),
    )(z_line)
    plane = gather_all(copies, "x")
    k_turned, v_aug, d_turned, d_extra = pl.pallas_call(
        assemble_kernel,
        out_shape=[
            jax.ShapeDtypeStruct((2 * HEAD, KEYS), jnp.bfloat16),
            jax.ShapeDtypeStruct((KEYS, 2 * HEAD), jnp.bfloat16),
            jax.ShapeDtypeStruct((HEAD, HEAD), jnp.float32),
            jax.ShapeDtypeStruct((rows, HEAD), jnp.float32),
        ],
        in_specs=[SMEM, SMEM] + [VMEM] * 4,
        out_specs=[VMEM] * 4,
        scratch_shapes=[
            pltpu.VMEM((KEYS, 2 * HEAD), jnp.bfloat16),
            pltpu.VMEM((rows, 2 * HEAD), jnp.bfloat16),
            pltpu.VMEM((rows, 2 * HEAD), jnp.float32),
            pltpu.VMEM((rows, HEAD), jnp.float32),
        ],
        compiler_params=params(),
        cost_estimate=cost(256, KEYS),
    )(rank, reach, entry_bias, d_aug, d_acc, plane)

    answers = {}
    for by in (2, 1, 3, 0):
        own = [own_kv] if by == 0 else []
        kind = jnp.float32 if by == 0 else jnp.bfloat16
        answer = pl.pallas_call(
            functools.partial(group_kernel, by),
            out_shape=jax.ShapeDtypeStruct((2 * HALF, WIDE), kind),
            in_specs=[SMEM] + [VMEM] * (5 + len(own)),
            out_specs=VMEM,
            scratch_shapes=[
                pltpu.VMEM((PROMPT_ROWS, 2 * HEAD), jnp.bfloat16),
                pltpu.VMEM((PROMPT_ROWS, 2 * HEAD), jnp.float32),
                pltpu.VMEM((PROMPT_ROWS, HEAD), jnp.float32),
            ]
            + [pltpu.VMEM((PROMPT_ROWS, 2 * HEAD), jnp.float32)] * len(own),
            compiler_params=params(),
            cost_estimate=cost(PROMPT_ROWS, KEYS),
        )(reach, queries[by], k_turned, v_aug, d_turned, d_extra, *own)
        answers[by] = answer if by == 0 else rotate(answer, "y", SIDE - by)
    partial = [answers[by] for by in range(SIDE)]
    decoded = pl.pallas_call(
        merge_decode_kernel,
        out_shape=jax.ShapeDtypeStruct((2, GROUP * HEAD), jnp.bfloat16),
        in_specs=[VMEM] * SIDE,
        out_specs=VMEM,
        compiler_params=params(),
        cost_estimate=cost(16, 64),
    )(*partial)
    decoded = lax.ppermute(decoded, "grp", [(0, 1), (1, 0)])
    prompt_attended = pl.pallas_call(
        merge_kernel,
        out_shape=jax.ShapeDtypeStruct((1, 2 * HALF, GROUP * HEAD), jnp.bfloat16),
        in_specs=[VMEM] * SIDE,
        out_specs=VMEM,
        compiler_params=params(),
        cost_estimate=cost(128, 512),
    )(*partial)
    step_attended = decoded.reshape(1, 2, 1, GROUP * HEAD)
    return prompt_attended, step_attended


def solution(mesh):
    pools, _, heads = mesh.devices.shape
    fine = Mesh(
        mesh.devices.reshape(pools, SIDE, SIDE, SIDE, heads), ("grp", "y", "x", "z", "tp")
    )
    seq = ("y", "x", "z")
    in_specs = (
        P("grp", seq, "tp"),
        P("grp", seq, "tp"),
        P("grp", seq, "tp"),
        P("grp", None, None, "tp"),
        P("grp", None, None, "tp"),
        P("grp", None, None, "tp"),
        P("grp", None),
        P(),
        P(),
    )
    out_specs = (P("grp", seq, "tp"), P("grp", None, seq, "tp"))
    return jax.shard_map(
        per_device, mesh=fine, in_specs=in_specs, out_specs=out_specs, check_vma=False
    )
```

```python
import functools
import math

import jax
import jax.numpy as jnp
from jax import lax
from jax.experimental import pallas as pl
from jax.experimental.pallas import tpu as pltpu
from jax.sharding import Mesh, PartitionSpec as P

HEAD = 128
HALF = 64
GROUP = 8
SIDE = 4
SPAN = GROUP * HALF
PROMPT_ROWS = 2 * SPAN
DECODE_ROWS = 16
NEAR = 16
KEYS = NEAR * 2 * HALF
TILE_BLOCKS = 8
TILE = TILE_BLOCKS * HALF
PART = 256
MESSAGE = 48
OFFSET_LANE = 72
TURNED_LANE = 8
DECODE_LANE = 96
WIDE = GROUP * HEAD + HEAD
NEG = -1e30
SCALE2 = math.log2(math.e) / math.sqrt(HEAD)
VMEM_BYTES = 24 * 1024 * 1024

VMEM = pl.BlockSpec(memory_space=pltpu.VMEM)
SMEM = pl.BlockSpec(memory_space=pltpu.SMEM)
ANY = pl.BlockSpec(memory_space=pl.ANY)
NT = (((1,), (1,)), ((), ()))


def params():
    return pltpu.CompilerParams(vmem_limit_bytes=VMEM_BYTES)


def cost(rows, keys):
    return pl.CostEstimate(
        flops=4 * rows * keys * 256,
        bytes_accessed=keys * 512 + rows * 2048,
        transcendentals=rows * keys,
    )


def scores_of(queries, keys):
    return lax.dot_general(queries, keys, NT, preferred_element_type=jnp.float32)


def back(at, by):
    return (at + SIDE - by) & (SIDE - 1)


def device_of(y, x, z):
    return (y * SIDE + x) * SIDE + z


def seq_position():
    return lax.axis_index("y"), lax.axis_index("x"), lax.axis_index("z")


def start_and_wait(copies):
    for copy in copies:
        copy.start()
    for copy in copies:
        copy.wait()


def copy_kernel(block, copies, sems):
    start_and_wait(
        [
            pltpu.make_async_copy(block, copies.at[place], sems.at[place])
            for place in range(SIDE)
        ]
    )


def pack_kernel(queries, keys, values, lengths, message, rows):
    y, x, z = seq_position()
    rows[...] = jnp.zeros_like(rows)
    lane = lax.broadcasted_iota(jnp.int32, (1, HEAD), 1)
    for by in range(SIDE):
        mine = device_of(back(y, by), x, z)
        top = by * MESSAGE
        for step in range(2):
            block = queries[0, step].astype(jnp.float32)
            here = lax.broadcasted_iota(jnp.int32, block.shape, 0) == mine
            line = jnp.sum(jnp.where(here, block, 0.0), axis=0, keepdims=True)
            for head in range(GROUP):
                at = top + step * GROUP + head
                rows[at : at + 1, :] = line[:, head * HEAD : (head + 1) * HEAD]
            for source, first in ((keys, 16), (values, 32)):
                block = source[0, step].astype(jnp.float32)
                here = lax.broadcasted_iota(jnp.int32, block.shape, 0) == mine
                at = top + first + step
                rows[at : at + 1, :] = jnp.sum(
                    jnp.where(here, block, 0.0), axis=0, keepdims=True
                )
        length = lengths[0, mine]
        digits = jnp.where(lane == 0, length >> 7, jnp.where(lane == 1, length & 127, 0))
        rows[top + 47 : top + 48, :] = digits.astype(jnp.float32)
    message[...] = rows[...].astype(jnp.bfloat16)


def prepare_kernel(order, message, owners, entry_bias, d_aug, d_acc, rank, reach, table):
    y, x, z = seq_position()
    pool = lax.axis_index("grp")
    places = 2 * SIDE * NEAR
    for place in range(places):
        table[place] = 0
    spots = [order[pool, 2 * NEAR * y + block] for block in range(2 * NEAR)]
    for spot in spots:
        table[spot] = 1
    below = jnp.int32(0)
    for place in range(places):
        taken = table[place]
        table[place] = below
        below = below + taken
    for block in range(2 * NEAR):
        rank[block] = table[spots[block]]
    for by in range(SIDE):
        for half in range(2):
            limit = order[pool, 2 * device_of(back(y, by), x, z) + half]
            reach[2 * by + half] = table[limit]

    lane16 = lax.broadcasted_iota(jnp.int32, (DECODE_ROWS, HEAD), 1)
    last = lax.broadcasted_iota(jnp.int32, (DECODE_ROWS, HEAD), 0) == 15
    step = lax.broadcasted_iota(jnp.int32, (16, 16), 0) >> 3
    known = lax.broadcasted_iota(jnp.int32, (16, 16), 1) <= step
    digit_worth = jnp.where(lane16 == 0, 128.0, jnp.where(lane16 == 1, 1.0, 0.0))
    page = lax.broadcasted_iota(jnp.int32, (64, 64), 0) * 64 + lax.broadcasted_iota(
        jnp.int32, (64, 64), 1
    )
    rank_key = owners[...] * 4096 + page
    packed_key = jnp.concatenate([rank_key[0:32], rank_key[32:64]], axis=1)
    token = lax.broadcasted_iota(jnp.int32, (2 * HALF, 64), 0)
    of_page = lax.broadcasted_iota(jnp.int32, (2 * HALF, 64), 1)
    spread = [
        jnp.where(token == 2 * of_page + odd, 1.0, 0.0).astype(jnp.bfloat16) for odd in range(2)
    ]
    device = lax.broadcasted_iota(jnp.int32, (64, HEAD), 0)
    lane = lax.broadcasted_iota(jnp.int32, (64, HEAD), 1)
    wanted, excess = [], []
    for by in range(SIDE):
        top = by * MESSAGE
        rows = slice(by * DECODE_ROWS, (by + 1) * DECODE_ROWS)
        d_aug[rows, 0:HEAD] = message[top : top + 16, :]
        fresh = scores_of(message[top : top + 16, :], message[top + 16 : top + 32, :])
        fresh = jnp.where(known, fresh, NEG)
        offset = jnp.max(fresh, axis=1, keepdims=True).astype(jnp.bfloat16).astype(jnp.float32)
        d_aug[rows, HEAD : 2 * HEAD] = jnp.where(
            (lane16 >> 4) == by, 1.0, jnp.where(lane16 == OFFSET_LANE, offset, 0.0)
        ).astype(jnp.bfloat16)
        if by == 0:
            weights = jnp.exp2((fresh - offset) * SCALE2)
            d_acc[rows, 0:HEAD] = jnp.dot(
                weights.astype(jnp.bfloat16),
                message[top + 32 : top + 48, :],
                preferred_element_type=jnp.float32,
            )
            d_acc[rows, HEAD : 2 * HEAD] = jnp.broadcast_to(
                jnp.sum(weights, axis=1, keepdims=True), (DECODE_ROWS, HEAD)
            )
        else:
            d_acc[rows, :] = jnp.zeros((DECODE_ROWS, 2 * HEAD), jnp.float32)
        digits = message[top + 32 : top + 48, :].astype(jnp.float32)
        length = jnp.sum(jnp.where(last, digits * digit_worth, 0.0), axis=(0, 1), keepdims=True)
        length = length.astype(jnp.int32)
        wanted.append((length >> 1).astype(jnp.float32))
        excess.append(length & 1)
    bound = [jnp.zeros((1, 1), jnp.int32) for _ in wanted]
    for bit in range(18, -1, -1):
        for by in range(SIDE):
            trial = bound[by] + (1 << bit)
            under = jnp.sum(jnp.where(packed_key < trial, 1.0, 0.0), axis=(0, 1), keepdims=True)
            bound[by] = jnp.where(under <= wanted[by], trial, bound[by])
    read = jnp.zeros((2 * HALF, HEAD), jnp.float32)
    for by in range(SIDE):
        allowed = jnp.zeros((2 * HALF, 64), jnp.float32)
        for odd, limit in ((0, bound[by] + excess[by]), (1, bound[by])):
            some = jnp.where(rank_key < limit, 1.0, 0.0).astype(jnp.bfloat16)
            allowed += scores_of(spread[odd], some)
        place = jnp.where(
            ((lane >> 4) == by) & (device == NEAR * y + (lane & 15)), 1.0, 0.0
        ).astype(jnp.bfloat16)
        read += jnp.dot(allowed.astype(jnp.bfloat16), place, preferred_element_type=jnp.float32)
    lanes = lax.broadcasted_iota(jnp.int32, (2 * HALF, HEAD), 1)
    entry_bias[...] = jnp.where(lanes < 64, (1.0 - read) * NEG, 0.0)


def raise_offsets(q_aug, acc, peak, count):
    part = min(count, PART)
    for first in range(0, count, part):
        rows = slice(first, first + part)
        lane = lax.broadcasted_iota(jnp.int32, (part, HEAD), 1)
        tags = q_aug[rows, HEAD : 2 * HEAD].astype(jnp.float32)
        old = jnp.sum(jnp.where(lane == OFFSET_LANE, tags, 0.0), axis=1, keepdims=True)
        offset = (old + peak[rows, :]).astype(jnp.bfloat16).astype(jnp.float32)
        shrink = jnp.exp2((old - offset) * SCALE2)
        q_aug[rows, HEAD : 2 * HEAD] = jnp.where(lane == OFFSET_LANE, offset, tags).astype(
            jnp.bfloat16
        )
        acc[rows, 0:HEAD] = acc[rows, 0:HEAD] * shrink
        acc[rows, HEAD : 2 * HEAD] = acc[rows, HEAD : 2 * HEAD] * shrink


def attend(q_aug, acc, k_turned, v_aug, peak, rows, tile):
    keys = pl.ds(tile * TILE if isinstance(tile, int) else pl.multiple_of(tile * TILE, TILE), TILE)
    scores = jnp.dot(q_aug[rows, :], k_turned[:, keys], preferred_element_type=jnp.float32)
    if peak is not None:
        peak[rows, :] = jnp.maximum(peak[rows, :], jnp.max(scores, axis=1, keepdims=True))
    else:
        weights = jnp.exp2(scores * SCALE2).astype(jnp.bfloat16)
        acc[rows, :] += jnp.dot(weights, v_aug[keys, :], preferred_element_type=jnp.float32)


def outgrown(acc):
    return jnp.max(jnp.where(acc[:, HEAD : 2 * HEAD] < 1e30, 0.0, 1.0)) > 0.5


def sweep_prompt(q_aug, acc, k_turned, v_aug, peak, begin, ends):
    near_end = jnp.maximum(jnp.minimum(ends[0], ends[1]), begin)
    far_end = jnp.maximum(ends[0], ends[1])
    longer = jnp.where(ends[1] > ends[0], SPAN, 0)

    def both(tile, carry):
        for first in range(0, PROMPT_ROWS, SPAN):
            attend(q_aug, acc, k_turned, v_aug, peak, pl.ds(first, SPAN), tile)
        return carry

    def one(tile, carry):
        for first in range(0, SPAN, PART):
            rows = pl.ds(pl.multiple_of(longer + first, PART), PART)
            attend(q_aug, acc, k_turned, v_aug, peak, rows, tile)
        return carry

    lax.fori_loop(begin, near_end, both, 0)
    lax.fori_loop(near_end, far_end, one, 0)


def assemble_kernel(
    rank, reach, entry_bias, d_in, d_base, plane, k_turned, v_aug, d_turned, d_extra, k_aug, d_aug, d_acc, peak
):
    lane = lax.broadcasted_iota(jnp.int32, (HALF, HEAD), 1)
    row = lax.broadcasted_iota(jnp.int32, (1, HEAD), 1)
    ones = jnp.ones((HALF, HEAD), jnp.bfloat16)
    for at_x in range(SIDE):
        for at_z in range(SIDE):
            j = at_x * SIDE + at_z
            for half in range(2):
                slot = rank[2 * j + half]
                base = jnp.where(row == OFFSET_LANE, -1.0, 0.0)
                for number in range(2 * SIDE):
                    blocked = jnp.where(slot < reach[number], 0.0, NEG)
                    base = jnp.where(row == 64 + number, blocked, base)
                tokens = slice(half * HALF, (half + 1) * HALF)
                mask = jnp.where(
                    ((lane & 15) == j) & (lane < 64), entry_bias[tokens, :], base
                )
                at = pl.ds(pl.multiple_of(slot * HALF, HALF), HALF)
                k_aug[at, 0:HEAD] = plane[at_x, at_z, tokens, 0:HEAD]
                k_aug[at, HEAD : 2 * HEAD] = mask.astype(jnp.bfloat16)
                v_aug[at, 0:HEAD] = plane[at_x, at_z, tokens, HEAD : 2 * HEAD]
                v_aug[at, HEAD : 2 * HEAD] = ones
    for first in range(0, KEYS, 2 * HEAD):
        some = slice(first, first + 2 * HEAD)
        k_turned[:, some] = k_aug[some, :].T
    d_aug[...] = d_in[...]
    d_acc[...] = d_base[...]
    rows = SIDE * DECODE_ROWS

    def sweep(peak):
        for tile in range(KEYS // TILE):
            attend(d_aug, d_acc, k_turned, v_aug, peak, slice(0, rows), tile)

    sweep(None)

    @pl.when(outgrown(d_acc))
    def _():
        peak[...] = jnp.zeros_like(peak)
        sweep(peak)
        d_acc[...] = d_base[...]
        raise_offsets(d_aug, d_acc, peak, rows)
        sweep(None)

    total = d_acc[:, HEAD : 2 * HEAD]
    tags = d_aug[:, HEAD : 2 * HEAD].astype(jnp.float32)
    wide = lax.broadcasted_iota(jnp.int32, (rows, HEAD), 1)
    offset = jnp.sum(jnp.where(wide == OFFSET_LANE, tags, 0.0), axis=1, keepdims=True)
    answer = d_acc[:, 0:HEAD] / jnp.maximum(total, 1e-30)
    d_turned[...] = jnp.concatenate([answer, jnp.zeros((HEAD - rows, HEAD), jnp.float32)]).T
    high = total.astype(jnp.bfloat16).astype(jnp.float32)
    d_extra[...] = jnp.where(
        wide == DECODE_LANE,
        high,
        jnp.where(
            wide == DECODE_LANE + 1,
            total - high,
            jnp.where(wide == DECODE_LANE + 2, offset, 0.0),
        ),
    )


def group_kernel(by, reach, queries, k_turned, v_aug, d_turned, d_extra, *refs):
    if by == 0:
        own_kv, answer, q_aug, acc, peak, base = refs
    else:
        answer, q_aug, acc, peak = refs
    reached = [reach[2 * by + block] for block in range(2)]
    ends = [(count + TILE_BLOCKS - 1) // TILE_BLOCKS for count in reached]
    for block in range(2):
        tokens = slice(block * HALF, (block + 1) * HALF)
        rows = slice(block * SPAN, (block + 1) * SPAN)
        for head in range(GROUP):
            at = block * SPAN + head * HALF
            q_aug[at : at + HALF, 0:HEAD] = queries[tokens, head * HEAD : (head + 1) * HEAD]
        lane = lax.broadcasted_iota(jnp.int32, (PART, HEAD), 1)
        flag = jnp.where(lane == 64 + 2 * by + block, 1.0, 0.0)
        q_aug[rows, HEAD : 2 * HEAD] = jnp.concatenate([flag] * (SPAN // PART)).astype(
            jnp.bfloat16
        )
    for first in range(0, PROMPT_ROWS, PART):
        block = first // SPAN
        some = slice(first, first + PART)
        flag = jnp.where(lane == 64 + 2 * by + block, 1.0, 0.0)
        if by == 0:
            tokens = slice(block * HALF, (block + 1) * HALF)
            token = lax.broadcasted_iota(jnp.int32, (PART, HALF), 0) & (HALF - 1)
            column = lax.broadcasted_iota(jnp.int32, (PART, HALF), 1)
            scores = scores_of(q_aug[some, 0:HEAD], own_kv[tokens, 0:HEAD])
            scores = jnp.where(column <= token, scores, NEG)
            offset = jnp.max(scores, axis=1, keepdims=True).astype(jnp.bfloat16)
            offset = offset.astype(jnp.float32)
            weights = jnp.exp2((scores - offset) * SCALE2)
            left = jnp.dot(
                weights.astype(jnp.bfloat16),
                own_kv[tokens, HEAD : 2 * HEAD],
                preferred_element_type=jnp.float32,
            )
            right = jnp.broadcast_to(jnp.sum(weights, axis=1, keepdims=True), (PART, HEAD))
            for ref in (acc, base):
                ref[some, 0:HEAD] = left
                ref[some, HEAD : 2 * HEAD] = right
        else:
            scores = jnp.dot(
                q_aug[some, :], k_turned[:, 0:TILE], preferred_element_type=jnp.float32
            )
            offset = jnp.max(scores, axis=1, keepdims=True).astype(jnp.bfloat16)
            offset = offset.astype(jnp.float32)
            weights = jnp.exp2((scores - offset) * SCALE2).astype(jnp.bfloat16)
            acc[some, :] = jnp.dot(
                weights, v_aug[0:TILE, :], preferred_element_type=jnp.float32
            ) * jnp.where(reached[block] > 0, 1.0, 0.0)
        q_aug[some, HEAD : 2 * HEAD] = jnp.where(lane == OFFSET_LANE, offset, flag).astype(
            jnp.bfloat16
        )

    sweep_prompt(q_aug, acc, k_turned, v_aug, None, 0 if by == 0 else 1, ends)

    @pl.when(outgrown(acc))
    def _():
        peak[...] = jnp.zeros_like(peak)
        sweep_prompt(q_aug, acc, k_turned, v_aug, peak, 0, ends)
        acc[...] = base[...] if by == 0 else jnp.zeros_like(acc)
        raise_offsets(q_aug, acc, peak, PROMPT_ROWS)
        sweep_prompt(q_aug, acc, k_turned, v_aug, None, 0, ends)

    wide = lax.broadcasted_iota(jnp.int32, (HALF, HEAD), 1)
    for block in range(2):
        tokens = slice(block * HALF, (block + 1) * HALF)
        turned = pltpu.roll(
            d_turned[tokens, :], (HEAD + TURNED_LANE - DECODE_ROWS * by) % HEAD, 1
        )
        extra = jnp.where(
            (wide >= TURNED_LANE) & (wide < TURNED_LANE + DECODE_ROWS), turned, 0.0
        )
        if block == 0:
            mine = d_extra[by * DECODE_ROWS : (by + 1) * DECODE_ROWS, :]
            rest = jnp.zeros((HALF - DECODE_ROWS, HEAD), jnp.float32)
            extra = extra + jnp.concatenate([mine, rest])
        for head in range(GROUP):
            at = block * SPAN + head * HALF
            rows = slice(at, at + HALF)
            total = acc[rows, HEAD : 2 * HEAD]
            tags = q_aug[rows, HEAD : 2 * HEAD].astype(jnp.float32)
            offset = jnp.sum(jnp.where(wide == OFFSET_LANE, tags, 0.0), axis=1, keepdims=True)
            high = total.astype(jnp.bfloat16).astype(jnp.float32)
            extra = jnp.where(wide == head, high, extra)
            extra = jnp.where(wide == 32 + head, total - high, extra)
            extra = jnp.where(wide == 64 + head, offset, extra)
            answer[tokens, head * HEAD : (head + 1) * HEAD] = (
                acc[rows, 0:HEAD] / jnp.maximum(total, 1e-30)
            ).astype(answer.dtype)
        answer[tokens, GROUP * HEAD : WIDE] = extra.astype(answer.dtype)


def groups_kernel(distances, reach, *refs):
    number = len(distances)
    queries, shared, rest = refs[:number], refs[number : number + 4], refs[number + 4 :]
    for by, asked, answer in zip(distances, queries, rest[:number]):
        group_kernel(by, reach, asked, *shared, answer, *rest[number:])


def shares(extras):
    extras = [extra.astype(jnp.float32) for extra in extras]
    totals = [extra + pltpu.roll(extra, HEAD - 32, 1) for extra in extras]
    offsets = [pltpu.roll(extra, HEAD - 64, 1) for extra in extras]
    top = functools.reduce(jnp.maximum, offsets)
    parts = [total * jnp.exp2((offset - top) * SCALE2) for total, offset in zip(totals, offsets)]
    whole = functools.reduce(jnp.add, parts)
    return [part / whole for part in parts]


def merge_decode_kernel(*refs):
    answers, decode_out = refs[:SIDE], refs[SIDE]
    columns = [answer[:, GROUP * HEAD : WIDE].astype(jnp.float32) for answer in answers]
    firsts = [column[0:DECODE_ROWS] for column in columns]
    at = DECODE_LANE
    totals = [first[:, at : at + 1] + first[:, at + 1 : at + 2] for first in firsts]
    offsets = [first[:, at + 2 : at + 3] for first in firsts]
    top = functools.reduce(jnp.maximum, offsets)
    parts = [total * jnp.exp2((offset - top) * SCALE2) for total, offset in zip(totals, offsets)]
    whole = functools.reduce(jnp.add, parts)
    merged = functools.reduce(
        jnp.add,
        [
            column.T[TURNED_LANE : TURNED_LANE + DECODE_ROWS] * (part / whole)
            for column, part in zip(columns, parts)
        ],
    )
    for head in range(GROUP):
        steps = [merged[at : at + 1] for at in (head, GROUP + head)]
        decode_out[:, head * HEAD : (head + 1) * HEAD] = jnp.concatenate(steps, axis=0).astype(
            jnp.bfloat16
        )


def merge_kernel(*refs):
    answers, prompt_out = refs[:SIDE], refs[SIDE]
    for block in range(2):
        tokens = slice(block * HALF, (block + 1) * HALF)
        parts = shares([answer[tokens, GROUP * HEAD : WIDE] for answer in answers])
        for head in range(GROUP):
            lanes = slice(head * HEAD, (head + 1) * HEAD)
            prompt_out[0, tokens, lanes] = functools.reduce(
                jnp.add,
                [
                    answer[tokens, lanes].astype(jnp.float32) * part[:, head : head + 1]
                    for answer, part in zip(answers, parts)
                ],
            ).astype(jnp.bfloat16)


def rotate(block, axis, by):
    return lax.ppermute(block, axis, [(i, (i + by) % SIDE) for i in range(SIDE)])


def gather_all(copies, axis):
    return lax.all_to_all(copies, axis, split_axis=0, concat_axis=0, tiled=True)


def per_device(
    prompt_queries,
    prompt_keys,
    prefill_value_rows,
    step_queries,
    step_keys,
    decode_step_values,
    context_lengths,
    span_order,
    page_owner,
):
    own_kv = jnp.concatenate([prompt_keys[0], prefill_value_rows[0]], axis=1)
    copies = jnp.broadcast_to(own_kv[None], (SIDE,) + own_kv.shape)
    z_line = gather_all(copies, "z")
    message = pl.pallas_call(
        pack_kernel,
        out_shape=jax.ShapeDtypeStruct((SIDE * MESSAGE, HEAD), jnp.bfloat16),
        in_specs=[VMEM, VMEM, VMEM, SMEM],
        out_specs=VMEM,
        scratch_shapes=[pltpu.VMEM((SIDE * MESSAGE, HEAD), jnp.float32)],
        compiler_params=params(),
    )(step_queries, step_keys, decode_step_values, context_lengths)
    message = lax.ppermute(message, "grp", [(0, 1), (1, 0)])
    pool = lax.axis_index("grp")
    owners = lax.dynamic_index_in_dim(page_owner, pool, 0, keepdims=False).reshape(64, 64)
    rows = SIDE * DECODE_ROWS
    entry_bias, d_aug, d_acc, rank, reach = pl.pallas_call(
        prepare_kernel,
        out_shape=[
            jax.ShapeDtypeStruct((2 * HALF, HEAD), jnp.float32),
            jax.ShapeDtypeStruct((rows, 2 * HEAD), jnp.bfloat16),
            jax.ShapeDtypeStruct((rows, 2 * HEAD), jnp.float32),
            jax.ShapeDtypeStruct((2 * NEAR,), jnp.int32),
            jax.ShapeDtypeStruct((2 * SIDE,), jnp.int32),
        ],
        in_specs=[SMEM, VMEM, VMEM],
        out_specs=[VMEM, VMEM, VMEM, SMEM, SMEM],
        scratch_shapes=[pltpu.SMEM((2 * SIDE * NEAR,), jnp.int32)],
        compiler_params=params(),
        cost_estimate=cost(1024, 512),
    )(span_order, message, owners)
    z_line, entry_bias, sent_queries = lax.optimization_barrier(
        (z_line, entry_bias, prompt_queries[0])
    )
    queries = {by: rotate(sent_queries, "y", by) for by in (2, 1, 3)}
    queries[0] = prompt_queries[0]
    copies = pl.pallas_call(
        copy_kernel,
        out_shape=jax.ShapeDtypeStruct((SIDE,) + z_line.shape, jnp.bfloat16),
        in_specs=[ANY],
        out_specs=ANY,
        scratch_shapes=[pltpu.SemaphoreType.DMA((SIDE,))],
        compiler_params=params(),
    )(z_line)
    plane = gather_all(copies, "x")
    k_turned, v_aug, d_turned, d_extra = pl.pallas_call(
        assemble_kernel,
        out_shape=[
            jax.ShapeDtypeStruct((2 * HEAD, KEYS), jnp.bfloat16),
            jax.ShapeDtypeStruct((KEYS, 2 * HEAD), jnp.bfloat16),
            jax.ShapeDtypeStruct((HEAD, HEAD), jnp.float32),
            jax.ShapeDtypeStruct((rows, HEAD), jnp.float32),
        ],
        in_specs=[SMEM, SMEM] + [VMEM] * 4,
        out_specs=[VMEM] * 4,
        scratch_shapes=[
            pltpu.VMEM((KEYS, 2 * HEAD), jnp.bfloat16),
            pltpu.VMEM((rows, 2 * HEAD), jnp.bfloat16),
            pltpu.VMEM((rows, 2 * HEAD), jnp.float32),
            pltpu.VMEM((rows, HEAD), jnp.float32),
        ],
        compiler_params=params(),
        cost_estimate=cost(256, KEYS),
    )(rank, reach, entry_bias, d_aug, d_acc, plane)

    scratch = [
        pltpu.VMEM((PROMPT_ROWS, 2 * HEAD), jnp.bfloat16),
        pltpu.VMEM((PROMPT_ROWS, 2 * HEAD), jnp.float32),
        pltpu.VMEM((PROMPT_ROWS, HEAD), jnp.float32),
    ]
    shared = (k_turned, v_aug, d_turned, d_extra)
    answers = {}
    for distances in ((2,), (3, 1)):
        found = pl.pallas_call(
            functools.partial(groups_kernel, distances),
            out_shape=[jax.ShapeDtypeStruct((2 * HALF, WIDE), jnp.bfloat16) for _ in distances],
            in_specs=[SMEM] + [VMEM] * (len(distances) + len(shared)),
            out_specs=[VMEM] * len(distances),
            scratch_shapes=scratch,
            compiler_params=params(),
            cost_estimate=cost(len(distances) * PROMPT_ROWS, KEYS),
        )(reach, *[queries[by] for by in distances], *shared)
        for by, answer in zip(distances, found):
            answers[by] = rotate(answer, "y", SIDE - by)
    answers[0] = pl.pallas_call(
        functools.partial(group_kernel, 0),
        out_shape=jax.ShapeDtypeStruct((2 * HALF, WIDE), jnp.float32),
        in_specs=[SMEM] + [VMEM] * (2 + len(shared)),
        out_specs=VMEM,
        scratch_shapes=scratch + [pltpu.VMEM((PROMPT_ROWS, 2 * HEAD), jnp.float32)],
        compiler_params=params(),
        cost_estimate=cost(PROMPT_ROWS, KEYS),
    )(reach, queries[0], *shared, own_kv)
    partial = [answers[by] for by in range(SIDE)]
    decoded = pl.pallas_call(
        merge_decode_kernel,
        out_shape=jax.ShapeDtypeStruct((2, GROUP * HEAD), jnp.bfloat16),
        in_specs=[VMEM] * SIDE,
        out_specs=VMEM,
        compiler_params=params(),
        cost_estimate=cost(16, 64),
    )(*partial)
    decoded = lax.ppermute(decoded, "grp", [(0, 1), (1, 0)])
    prompt_attended = pl.pallas_call(
        merge_kernel,
        out_shape=jax.ShapeDtypeStruct((1, 2 * HALF, GROUP * HEAD), jnp.bfloat16),
        in_specs=[VMEM] * SIDE,
        out_specs=VMEM,
        compiler_params=params(),
        cost_estimate=cost(128, 512),
    )(*partial)
    step_attended = decoded.reshape(1, 2, 1, GROUP * HEAD)
    return prompt_attended, step_attended


def solution(mesh):
    pools, _, heads = mesh.devices.shape
    fine = Mesh(
        mesh.devices.reshape(pools, SIDE, SIDE, SIDE, heads), ("grp", "y", "x", "z", "tp")
    )
    seq = ("y", "x", "z")
    in_specs = (
        P("grp", seq, "tp"),
        P("grp", seq, "tp"),
        P("grp", seq, "tp"),
        P("grp", None, None, "tp"),
        P("grp", None, None, "tp"),
        P("grp", None, None, "tp"),
        P("grp", None),
        P(),
        P(),
    )
    out_specs = (P("grp", seq, "tp"), P("grp", None, seq, "tp"))
    return jax.shard_map(
        per_device, mesh=fine, in_specs=in_specs, out_specs=out_specs, check_vma=False
    )
```

```python
import functools
import math

import jax
import jax.numpy as jnp
from jax import lax
from jax.experimental import pallas as pl
from jax.experimental.pallas import tpu as pltpu
from jax.sharding import Mesh, PartitionSpec as P

HEAD = 128
HALF = 64
GROUP = 8
SIDE = 4
SPAN = GROUP * HALF
PROMPT_ROWS = 2 * SPAN
DECODE_ROWS = 16
NEAR = 16
KEYS = NEAR * 2 * HALF
TILE_BLOCKS = 8
TILE = TILE_BLOCKS * HALF
PART = 256
MESSAGE = 48
OFFSET_LANE = 72
TURNED_LANE = 8
DECODE_LANE = 96
WIDE = GROUP * HEAD + HEAD
NEG = -1e30
SCALE2 = math.log2(math.e) / math.sqrt(HEAD)
VMEM_BYTES = 24 * 1024 * 1024

VMEM = pl.BlockSpec(memory_space=pltpu.VMEM)
SMEM = pl.BlockSpec(memory_space=pltpu.SMEM)
ANY = pl.BlockSpec(memory_space=pl.ANY)
NT = (((1,), (1,)), ((), ()))


def params():
    return pltpu.CompilerParams(vmem_limit_bytes=VMEM_BYTES)


def cost(rows, keys):
    return pl.CostEstimate(
        flops=4 * rows * keys * 256,
        bytes_accessed=keys * 512 + rows * 2048,
        transcendentals=rows * keys,
    )


def scores_of(queries, keys):
    return lax.dot_general(queries, keys, NT, preferred_element_type=jnp.float32)


def back(at, by):
    return (at + SIDE - by) & (SIDE - 1)


def device_of(y, x, z):
    return (y * SIDE + x) * SIDE + z


def seq_position():
    return lax.axis_index("y"), lax.axis_index("x"), lax.axis_index("z")


def start_and_wait(copies):
    for copy in copies:
        copy.start()
    for copy in copies:
        copy.wait()


def copy_kernel(block, copies, sems):
    start_and_wait(
        [
            pltpu.make_async_copy(block, copies.at[place], sems.at[place])
            for place in range(SIDE)
        ]
    )


def pack_kernel(queries, keys, values, lengths, message, rows):
    y, x, z = seq_position()
    rows[...] = jnp.zeros_like(rows)
    lane = lax.broadcasted_iota(jnp.int32, (1, HEAD), 1)
    for by in range(SIDE):
        mine = device_of(back(y, by), x, z)
        top = by * MESSAGE
        for step in range(2):
            block = queries[0, step].astype(jnp.float32)
            here = lax.broadcasted_iota(jnp.int32, block.shape, 0) == mine
            line = jnp.sum(jnp.where(here, block, 0.0), axis=0, keepdims=True)
            for head in range(GROUP):
                at = top + step * GROUP + head
                rows[at : at + 1, :] = line[:, head * HEAD : (head + 1) * HEAD]
            for source, first in ((keys, 16), (values, 32)):
                block = source[0, step].astype(jnp.float32)
                here = lax.broadcasted_iota(jnp.int32, block.shape, 0) == mine
                at = top + first + step
                rows[at : at + 1, :] = jnp.sum(
                    jnp.where(here, block, 0.0), axis=0, keepdims=True
                )
        length = lengths[0, mine]
        digits = jnp.where(lane == 0, length >> 7, jnp.where(lane == 1, length & 127, 0))
        rows[top + 47 : top + 48, :] = digits.astype(jnp.float32)
    message[...] = rows[...].astype(jnp.bfloat16)


def prepare_kernel(order, message, owners, entry_bias, d_aug, d_acc, rank, reach, table):
    y, x, z = seq_position()
    pool = lax.axis_index("grp")
    places = 2 * SIDE * NEAR
    for place in range(places):
        table[place] = 0
    spots = [order[pool, 2 * NEAR * y + block] for block in range(2 * NEAR)]
    for spot in spots:
        table[spot] = 1
    below = jnp.int32(0)
    for place in range(places):
        taken = table[place]
        table[place] = below
        below = below + taken
    for block in range(2 * NEAR):
        rank[block] = table[spots[block]]
    for by in range(SIDE):
        for half in range(2):
            limit = order[pool, 2 * device_of(back(y, by), x, z) + half]
            reach[2 * by + half] = table[limit]

    lane16 = lax.broadcasted_iota(jnp.int32, (DECODE_ROWS, HEAD), 1)
    last = lax.broadcasted_iota(jnp.int32, (DECODE_ROWS, HEAD), 0) == 15
    step = lax.broadcasted_iota(jnp.int32, (16, 16), 0) >> 3
    known = lax.broadcasted_iota(jnp.int32, (16, 16), 1) <= step
    digit_worth = jnp.where(lane16 == 0, 128.0, jnp.where(lane16 == 1, 1.0, 0.0))
    page = lax.broadcasted_iota(jnp.int32, (64, 64), 0) * 64 + lax.broadcasted_iota(
        jnp.int32, (64, 64), 1
    )
    rank_key = owners[...] * 4096 + page
    packed_key = jnp.concatenate([rank_key[0:32], rank_key[32:64]], axis=1)
    token = lax.broadcasted_iota(jnp.int32, (2 * HALF, 64), 0)
    of_page = lax.broadcasted_iota(jnp.int32, (2 * HALF, 64), 1)
    spread = [
        jnp.where(token == 2 * of_page + odd, 1.0, 0.0).astype(jnp.bfloat16) for odd in range(2)
    ]
    device = lax.broadcasted_iota(jnp.int32, (64, HEAD), 0)
    lane = lax.broadcasted_iota(jnp.int32, (64, HEAD), 1)
    wanted, excess = [], []
    for by in range(SIDE):
        top = by * MESSAGE
        rows = slice(by * DECODE_ROWS, (by + 1) * DECODE_ROWS)
        d_aug[rows, 0:HEAD] = message[top : top + 16, :]
        fresh = scores_of(message[top : top + 16, :], message[top + 16 : top + 32, :])
        fresh = jnp.where(known, fresh, NEG)
        offset = jnp.max(fresh, axis=1, keepdims=True).astype(jnp.bfloat16).astype(jnp.float32)
        d_aug[rows, HEAD : 2 * HEAD] = jnp.where(
            (lane16 >> 4) == by, 1.0, jnp.where(lane16 == OFFSET_LANE, offset, 0.0)
        ).astype(jnp.bfloat16)
        if by == 0:
            weights = jnp.exp2((fresh - offset) * SCALE2)
            d_acc[rows, 0:HEAD] = jnp.dot(
                weights.astype(jnp.bfloat16),
                message[top + 32 : top + 48, :],
                preferred_element_type=jnp.float32,
            )
            d_acc[rows, HEAD : 2 * HEAD] = jnp.broadcast_to(
                jnp.sum(weights, axis=1, keepdims=True), (DECODE_ROWS, HEAD)
            )
        else:
            d_acc[rows, :] = jnp.zeros((DECODE_ROWS, 2 * HEAD), jnp.float32)
        digits = message[top + 32 : top + 48, :].astype(jnp.float32)
        length = jnp.sum(jnp.where(last, digits * digit_worth, 0.0), axis=(0, 1), keepdims=True)
        length = length.astype(jnp.int32)
        wanted.append((length >> 1).astype(jnp.float32))
        excess.append(length & 1)
    bound = [jnp.zeros((1, 1), jnp.int32) for _ in wanted]
    for bit in range(18, -1, -1):
        for by in range(SIDE):
            trial = bound[by] + (1 << bit)
            under = jnp.sum(jnp.where(packed_key < trial, 1.0, 0.0), axis=(0, 1), keepdims=True)
            bound[by] = jnp.where(under <= wanted[by], trial, bound[by])
    read = jnp.zeros((2 * HALF, HEAD), jnp.float32)
    for by in range(SIDE):
        allowed = jnp.zeros((2 * HALF, 64), jnp.float32)
        for odd, limit in ((0, bound[by] + excess[by]), (1, bound[by])):
            some = jnp.where(rank_key < limit, 1.0, 0.0).astype(jnp.bfloat16)
            allowed += scores_of(spread[odd], some)
        place = jnp.where(
            ((lane >> 4) == by) & (device == NEAR * y + (lane & 15)), 1.0, 0.0
        ).astype(jnp.bfloat16)
        read += jnp.dot(allowed.astype(jnp.bfloat16), place, preferred_element_type=jnp.float32)
    lanes = lax.broadcasted_iota(jnp.int32, (2 * HALF, HEAD), 1)
    entry_bias[...] = jnp.where(lanes < 64, (1.0 - read) * NEG, 0.0)


def raise_offsets(q_aug, acc, peak, count):
    part = min(count, PART)
    for first in range(0, count, part):
        rows = slice(first, first + part)
        lane = lax.broadcasted_iota(jnp.int32, (part, HEAD), 1)
        tags = q_aug[rows, HEAD : 2 * HEAD].astype(jnp.float32)
        old = jnp.sum(jnp.where(lane == OFFSET_LANE, tags, 0.0), axis=1, keepdims=True)
        offset = (old + peak[rows, :]).astype(jnp.bfloat16).astype(jnp.float32)
        shrink = jnp.exp2((old - offset) * SCALE2)
        q_aug[rows, HEAD : 2 * HEAD] = jnp.where(lane == OFFSET_LANE, offset, tags).astype(
            jnp.bfloat16
        )
        acc[rows, 0:HEAD] = acc[rows, 0:HEAD] * shrink
        acc[rows, HEAD : 2 * HEAD] = acc[rows, HEAD : 2 * HEAD] * shrink


def attend(q_aug, acc, k_turned, v_aug, peak, rows, tile):
    keys = pl.ds(tile * TILE if isinstance(tile, int) else pl.multiple_of(tile * TILE, TILE), TILE)
    scores = jnp.dot(q_aug[rows, :], k_turned[:, keys], preferred_element_type=jnp.float32)
    if peak is not None:
        peak[rows, :] = jnp.maximum(peak[rows, :], jnp.max(scores, axis=1, keepdims=True))
    else:
        weights = jnp.exp2(scores * SCALE2).astype(jnp.bfloat16)
        acc[rows, :] += jnp.dot(weights, v_aug[keys, :], preferred_element_type=jnp.float32)


def outgrown(acc):
    return jnp.max(jnp.where(acc[:, HEAD : 2 * HEAD] < 1e30, 0.0, 1.0)) > 0.5


def sweep_prompt(q_aug, acc, k_turned, v_aug, peak, begin, ends):
    near_end = jnp.maximum(jnp.minimum(ends[0], ends[1]), begin)
    far_end = jnp.maximum(ends[0], ends[1])
    longer = jnp.where(ends[1] > ends[0], SPAN, 0)

    def both(tile, carry):
        for first in range(0, PROMPT_ROWS, SPAN):
            attend(q_aug, acc, k_turned, v_aug, peak, pl.ds(first, SPAN), tile)
        return carry

    def one(tile, carry):
        for first in range(0, SPAN, PART):
            rows = pl.ds(pl.multiple_of(longer + first, PART), PART)
            attend(q_aug, acc, k_turned, v_aug, peak, rows, tile)
        return carry

    lax.fori_loop(begin, near_end, both, 0)
    lax.fori_loop(near_end, far_end, one, 0)


def assemble_kernel(
    rank, reach, entry_bias, d_in, d_base, plane, k_turned, v_aug, d_turned, d_extra, k_aug, d_aug, d_acc, peak
):
    lane = lax.broadcasted_iota(jnp.int32, (HALF, HEAD), 1)
    row = lax.broadcasted_iota(jnp.int32, (1, HEAD), 1)
    ones = jnp.ones((HALF, HEAD), jnp.bfloat16)
    for at_x in range(SIDE):
        for at_z in range(SIDE):
            j = at_x * SIDE + at_z
            for half in range(2):
                slot = rank[2 * j + half]
                base = jnp.where(row == OFFSET_LANE, -1.0, 0.0)
                for number in range(2 * SIDE):
                    blocked = jnp.where(slot < reach[number], 0.0, NEG)
                    base = jnp.where(row == 64 + number, blocked, base)
                tokens = slice(half * HALF, (half + 1) * HALF)
                mask = jnp.where(
                    ((lane & 15) == j) & (lane < 64), entry_bias[tokens, :], base
                )
                at = pl.ds(pl.multiple_of(slot * HALF, HALF), HALF)
                k_aug[at, 0:HEAD] = plane[at_x, at_z, tokens, 0:HEAD]
                k_aug[at, HEAD : 2 * HEAD] = mask.astype(jnp.bfloat16)
                v_aug[at, 0:HEAD] = plane[at_x, at_z, tokens, HEAD : 2 * HEAD]
                v_aug[at, HEAD : 2 * HEAD] = ones
    for first in range(0, KEYS, 2 * HEAD):
        some = slice(first, first + 2 * HEAD)
        k_turned[:, some] = k_aug[some, :].T
    d_aug[...] = d_in[...]
    d_acc[...] = d_base[...]
    rows = SIDE * DECODE_ROWS

    def sweep(peak):
        for tile in range(KEYS // TILE):
            attend(d_aug, d_acc, k_turned, v_aug, peak, slice(0, rows), tile)

    sweep(None)

    @pl.when(outgrown(d_acc))
    def _():
        peak[...] = jnp.zeros_like(peak)
        sweep(peak)
        d_acc[...] = d_base[...]
        raise_offsets(d_aug, d_acc, peak, rows)
        sweep(None)

    total = d_acc[:, HEAD : 2 * HEAD]
    tags = d_aug[:, HEAD : 2 * HEAD].astype(jnp.float32)
    wide = lax.broadcasted_iota(jnp.int32, (rows, HEAD), 1)
    offset = jnp.sum(jnp.where(wide == OFFSET_LANE, tags, 0.0), axis=1, keepdims=True)
    answer = d_acc[:, 0:HEAD] / jnp.maximum(total, 1e-30)
    d_turned[...] = jnp.concatenate([answer, jnp.zeros((HEAD - rows, HEAD), jnp.float32)]).T
    high = total.astype(jnp.bfloat16).astype(jnp.float32)
    d_extra[...] = jnp.where(
        wide == DECODE_LANE,
        high,
        jnp.where(
            wide == DECODE_LANE + 1,
            total - high,
            jnp.where(wide == DECODE_LANE + 2, offset, 0.0),
        ),
    )


def group_kernel(by, reach, queries, k_turned, v_aug, d_turned, d_extra, *refs):
    if by == 0:
        own_kv, answer, q_aug, acc, peak, base = refs
    else:
        answer, q_aug, acc, peak = refs
    reached = [reach[2 * by + block] for block in range(2)]
    ends = [(count + TILE_BLOCKS - 1) // TILE_BLOCKS for count in reached]
    for block in range(2):
        tokens = slice(block * HALF, (block + 1) * HALF)
        rows = slice(block * SPAN, (block + 1) * SPAN)
        for head in range(GROUP):
            at = block * SPAN + head * HALF
            q_aug[at : at + HALF, 0:HEAD] = queries[tokens, head * HEAD : (head + 1) * HEAD]
        lane = lax.broadcasted_iota(jnp.int32, (PART, HEAD), 1)
        flag = jnp.where(lane == 64 + 2 * by + block, 1.0, 0.0)
        q_aug[rows, HEAD : 2 * HEAD] = jnp.concatenate([flag] * (SPAN // PART)).astype(
            jnp.bfloat16
        )
    for first in range(0, PROMPT_ROWS, PART):
        block = first // SPAN
        some = slice(first, first + PART)
        flag = jnp.where(lane == 64 + 2 * by + block, 1.0, 0.0)
        if by == 0:
            tokens = slice(block * HALF, (block + 1) * HALF)
            token = lax.broadcasted_iota(jnp.int32, (PART, HALF), 0) & (HALF - 1)
            column = lax.broadcasted_iota(jnp.int32, (PART, HALF), 1)
            scores = scores_of(q_aug[some, 0:HEAD], own_kv[tokens, 0:HEAD])
            scores = jnp.where(column <= token, scores, NEG)
            offset = jnp.max(scores, axis=1, keepdims=True).astype(jnp.bfloat16)
            offset = offset.astype(jnp.float32)
            weights = jnp.exp2((scores - offset) * SCALE2)
            left = jnp.dot(
                weights.astype(jnp.bfloat16),
                own_kv[tokens, HEAD : 2 * HEAD],
                preferred_element_type=jnp.float32,
            )
            right = jnp.broadcast_to(jnp.sum(weights, axis=1, keepdims=True), (PART, HEAD))
            for ref in (acc, base):
                ref[some, 0:HEAD] = left
                ref[some, HEAD : 2 * HEAD] = right
        else:
            scores = jnp.dot(
                q_aug[some, :], k_turned[:, 0:TILE], preferred_element_type=jnp.float32
            )
            offset = jnp.max(scores, axis=1, keepdims=True).astype(jnp.bfloat16)
            offset = offset.astype(jnp.float32)
            weights = jnp.exp2((scores - offset) * SCALE2).astype(jnp.bfloat16)
            acc[some, :] = jnp.dot(
                weights, v_aug[0:TILE, :], preferred_element_type=jnp.float32
            ) * jnp.where(reached[block] > 0, 1.0, 0.0)
        q_aug[some, HEAD : 2 * HEAD] = jnp.where(lane == OFFSET_LANE, offset, flag).astype(
            jnp.bfloat16
        )

    sweep_prompt(q_aug, acc, k_turned, v_aug, None, 0 if by == 0 else 1, ends)

    @pl.when(outgrown(acc))
    def _():
        peak[...] = jnp.zeros_like(peak)
        sweep_prompt(q_aug, acc, k_turned, v_aug, peak, 0, ends)
        acc[...] = base[...] if by == 0 else jnp.zeros_like(acc)
        raise_offsets(q_aug, acc, peak, PROMPT_ROWS)
        sweep_prompt(q_aug, acc, k_turned, v_aug, None, 0, ends)

    wide = lax.broadcasted_iota(jnp.int32, (HALF, HEAD), 1)
    for block in range(2):
        tokens = slice(block * HALF, (block + 1) * HALF)
        turned = pltpu.roll(
            d_turned[tokens, :], (HEAD + TURNED_LANE - DECODE_ROWS * by) % HEAD, 1
        )
        extra = jnp.where(
            (wide >= TURNED_LANE) & (wide < TURNED_LANE + DECODE_ROWS), turned, 0.0
        )
        if block == 0:
            mine = d_extra[by * DECODE_ROWS : (by + 1) * DECODE_ROWS, :]
            rest = jnp.zeros((HALF - DECODE_ROWS, HEAD), jnp.float32)
            extra = extra + jnp.concatenate([mine, rest])
        for head in range(GROUP):
            at = block * SPAN + head * HALF
            rows = slice(at, at + HALF)
            total = acc[rows, HEAD : 2 * HEAD]
            tags = q_aug[rows, HEAD : 2 * HEAD].astype(jnp.float32)
            offset = jnp.sum(jnp.where(wide == OFFSET_LANE, tags, 0.0), axis=1, keepdims=True)
            high = total.astype(jnp.bfloat16).astype(jnp.float32)
            extra = jnp.where(wide == head, high, extra)
            extra = jnp.where(wide == 32 + head, total - high, extra)
            extra = jnp.where(wide == 64 + head, offset, extra)
            answer[tokens, head * HEAD : (head + 1) * HEAD] = (
                acc[rows, 0:HEAD] / jnp.maximum(total, 1e-30)
            ).astype(answer.dtype)
        answer[tokens, GROUP * HEAD : WIDE] = extra.astype(answer.dtype)


def groups_kernel(distances, reach, *refs):
    number = len(distances)
    queries, shared, rest = refs[:number], refs[number : number + 4], refs[number + 4 :]
    for by, asked, answer in zip(distances, queries, rest[:number]):
        group_kernel(by, reach, asked, *shared, answer, *rest[number:])


def shares(extras):
    extras = [extra.astype(jnp.float32) for extra in extras]
    totals = [extra + pltpu.roll(extra, HEAD - 32, 1) for extra in extras]
    offsets = [pltpu.roll(extra, HEAD - 64, 1) for extra in extras]
    top = functools.reduce(jnp.maximum, offsets)
    parts = [total * jnp.exp2((offset - top) * SCALE2) for total, offset in zip(totals, offsets)]
    whole = functools.reduce(jnp.add, parts)
    return [part / whole for part in parts]


def merge_decode_kernel(*refs):
    answers, decode_out = refs[:SIDE], refs[SIDE]
    columns = [answer[:, GROUP * HEAD : WIDE].astype(jnp.float32) for answer in answers]
    firsts = [column[0:DECODE_ROWS] for column in columns]
    at = DECODE_LANE
    totals = [first[:, at : at + 1] + first[:, at + 1 : at + 2] for first in firsts]
    offsets = [first[:, at + 2 : at + 3] for first in firsts]
    top = functools.reduce(jnp.maximum, offsets)
    parts = [total * jnp.exp2((offset - top) * SCALE2) for total, offset in zip(totals, offsets)]
    whole = functools.reduce(jnp.add, parts)
    merged = functools.reduce(
        jnp.add,
        [
            column.T[TURNED_LANE : TURNED_LANE + DECODE_ROWS] * (part / whole)
            for column, part in zip(columns, parts)
        ],
    )
    for head in range(GROUP):
        steps = [merged[at : at + 1] for at in (head, GROUP + head)]
        decode_out[:, head * HEAD : (head + 1) * HEAD] = jnp.concatenate(steps, axis=0).astype(
            jnp.bfloat16
        )


def merge_kernel(*refs):
    answers, prompt_out = refs[:SIDE], refs[SIDE]
    for block in range(2):
        tokens = slice(block * HALF, (block + 1) * HALF)
        parts = shares([answer[tokens, GROUP * HEAD : WIDE] for answer in answers])
        for head in range(GROUP):
            lanes = slice(head * HEAD, (head + 1) * HEAD)
            prompt_out[0, tokens, lanes] = functools.reduce(
                jnp.add,
                [
                    answer[tokens, lanes].astype(jnp.float32) * part[:, head : head + 1]
                    for answer, part in zip(answers, parts)
                ],
            ).astype(jnp.bfloat16)


def rotate(block, axis, by):
    return lax.ppermute(block, axis, [(i, (i + by) % SIDE) for i in range(SIDE)])


def gather_all(copies, axis):
    return lax.all_to_all(copies, axis, split_axis=0, concat_axis=0, tiled=True)


def per_device(
    prompt_queries,
    prompt_keys,
    prefill_value_rows,
    step_queries,
    step_keys,
    decode_step_values,
    context_lengths,
    span_order,
    page_owner,
):
    own_kv = jnp.concatenate([prompt_keys[0], prefill_value_rows[0]], axis=1)
    copies = jnp.broadcast_to(own_kv[None], (SIDE,) + own_kv.shape)
    z_line = gather_all(copies, "z")
    message = pl.pallas_call(
        pack_kernel,
        out_shape=jax.ShapeDtypeStruct((SIDE * MESSAGE, HEAD), jnp.bfloat16),
        in_specs=[VMEM, VMEM, VMEM, SMEM],
        out_specs=VMEM,
        scratch_shapes=[pltpu.VMEM((SIDE * MESSAGE, HEAD), jnp.float32)],
        compiler_params=params(),
    )(step_queries, step_keys, decode_step_values, context_lengths)
    message = lax.ppermute(message, "grp", [(0, 1), (1, 0)])
    z_line, message, sent_queries = lax.optimization_barrier(
        (z_line, message, prompt_queries[0])
    )
    pool = lax.axis_index("grp")
    owners = lax.dynamic_index_in_dim(page_owner, pool, 0, keepdims=False).reshape(64, 64)
    rows = SIDE * DECODE_ROWS
    entry_bias, d_aug, d_acc, rank, reach = pl.pallas_call(
        prepare_kernel,
        out_shape=[
            jax.ShapeDtypeStruct((2 * HALF, HEAD), jnp.float32),
            jax.ShapeDtypeStruct((rows, 2 * HEAD), jnp.bfloat16),
            jax.ShapeDtypeStruct((rows, 2 * HEAD), jnp.float32),
            jax.ShapeDtypeStruct((2 * NEAR,), jnp.int32),
            jax.ShapeDtypeStruct((2 * SIDE,), jnp.int32),
        ],
        in_specs=[SMEM, VMEM, VMEM],
        out_specs=[VMEM, VMEM, VMEM, SMEM, SMEM],
        scratch_shapes=[pltpu.SMEM((2 * SIDE * NEAR,), jnp.int32)],
        compiler_params=params(),
        cost_estimate=cost(1024, 512),
    )(span_order, message, owners)
    queries = {by: rotate(sent_queries, "y", by) for by in (2, 1, 3)}
    queries[0] = prompt_queries[0]
    copies = pl.pallas_call(
        copy_kernel,
        out_shape=jax.ShapeDtypeStruct((SIDE,) + z_line.shape, jnp.bfloat16),
        in_specs=[ANY],
        out_specs=ANY,
        scratch_shapes=[pltpu.SemaphoreType.DMA((SIDE,))],
        compiler_params=params(),
    )(z_line)
    plane = gather_all(copies, "x")
    k_turned, v_aug, d_turned, d_extra = pl.pallas_call(
        assemble_kernel,
        out_shape=[
            jax.ShapeDtypeStruct((2 * HEAD, KEYS), jnp.bfloat16),
            jax.ShapeDtypeStruct((KEYS, 2 * HEAD), jnp.bfloat16),
            jax.ShapeDtypeStruct((HEAD, HEAD), jnp.float32),
            jax.ShapeDtypeStruct((rows, HEAD), jnp.float32),
        ],
        in_specs=[SMEM, SMEM] + [VMEM] * 4,
        out_specs=[VMEM] * 4,
        scratch_shapes=[
            pltpu.VMEM((KEYS, 2 * HEAD), jnp.bfloat16),
            pltpu.VMEM((rows, 2 * HEAD), jnp.bfloat16),
            pltpu.VMEM((rows, 2 * HEAD), jnp.float32),
            pltpu.VMEM((rows, HEAD), jnp.float32),
        ],
        compiler_params=params(),
        cost_estimate=cost(256, KEYS),
    )(rank, reach, entry_bias, d_aug, d_acc, plane)

    scratch = [
        pltpu.VMEM((PROMPT_ROWS, 2 * HEAD), jnp.bfloat16),
        pltpu.VMEM((PROMPT_ROWS, 2 * HEAD), jnp.float32),
        pltpu.VMEM((PROMPT_ROWS, HEAD), jnp.float32),
    ]
    shared = (k_turned, v_aug, d_turned, d_extra)
    answers = {}
    for distances in ((2,), (3, 1)):
        found = pl.pallas_call(
            functools.partial(groups_kernel, distances),
            out_shape=[jax.ShapeDtypeStruct((2 * HALF, WIDE), jnp.bfloat16) for _ in distances],
            in_specs=[SMEM] + [VMEM] * (len(distances) + len(shared)),
            out_specs=[VMEM] * len(distances),
            scratch_shapes=scratch,
            compiler_params=params(),
            cost_estimate=cost(len(distances) * PROMPT_ROWS, KEYS),
        )(reach, *[queries[by] for by in distances], *shared)
        for by, answer in zip(distances, found):
            answers[by] = rotate(answer, "y", SIDE - by)
    answers[0] = pl.pallas_call(
        functools.partial(group_kernel, 0),
        out_shape=jax.ShapeDtypeStruct((2 * HALF, WIDE), jnp.float32),
        in_specs=[SMEM] + [VMEM] * (2 + len(shared)),
        out_specs=VMEM,
        scratch_shapes=scratch + [pltpu.VMEM((PROMPT_ROWS, 2 * HEAD), jnp.float32)],
        compiler_params=params(),
        cost_estimate=cost(PROMPT_ROWS, KEYS),
    )(reach, queries[0], *shared, own_kv)
    partial = [answers[by] for by in range(SIDE)]
    decoded = pl.pallas_call(
        merge_decode_kernel,
        out_shape=jax.ShapeDtypeStruct((2, GROUP * HEAD), jnp.bfloat16),
        in_specs=[VMEM] * SIDE,
        out_specs=VMEM,
        compiler_params=params(),
        cost_estimate=cost(16, 64),
    )(*partial)
    decoded = lax.ppermute(decoded, "grp", [(0, 1), (1, 0)])
    prompt_attended = pl.pallas_call(
        merge_kernel,
        out_shape=jax.ShapeDtypeStruct((1, 2 * HALF, GROUP * HEAD), jnp.bfloat16),
        in_specs=[VMEM] * SIDE,
        out_specs=VMEM,
        compiler_params=params(),
        cost_estimate=cost(128, 512),
    )(*partial)
    step_attended = decoded.reshape(1, 2, 1, GROUP * HEAD)
    return prompt_attended, step_attended


def solution(mesh):
    pools, _, heads = mesh.devices.shape
    fine = Mesh(
        mesh.devices.reshape(pools, SIDE, SIDE, SIDE, heads), ("grp", "y", "x", "z", "tp")
    )
    seq = ("y", "x", "z")
    in_specs = (
        P("grp", seq, "tp"),
        P("grp", seq, "tp"),
        P("grp", seq, "tp"),
        P("grp", None, None, "tp"),
        P("grp", None, None, "tp"),
        P("grp", None, None, "tp"),
        P("grp", None),
        P(),
        P(),
    )
    out_specs = (P("grp", seq, "tp"), P("grp", None, seq, "tp"))
    return jax.shard_map(
        per_device, mesh=fine, in_specs=in_specs, out_specs=out_specs, check_vma=False
    )
```
